32 devices in a mesh: band: 4 (over z), grid: 8 (over y, x, core).
Axes of the slice: x: 2, y: 2, z: 4, core: 2. Of those that a mesh axis runs over, the one named last changes fastest.
Arguments:
- orbitals: float32 [16, 96, 9216], P('band', 'grid'), may hold values from -6 to 6
- pair_mask: int32 [16, 4], P('band'), may hold values 0 or 1
- cycle_step: int32 [], replicated, may hold values from 1 to 3
Outputs:
- exchange_field: float32 [16, 96, 9216], P('band', 'grid')
- projection: float32 [16, 4], P('band')
The draws below stay inside these ranges and needn't reach their ends.
All inputs are finite; a program needn't handle non-finite values. No bound on the sum of `pair_mask` on one device may be relied on, other than what follows from the above.
Results may differ from the reference program's by a relative error of at most 0.0003.
Values sent between devices are 32-bit elements; how exact they have to be, the bound alone decides.
No kernel may reach another device: no remote copies, remote signals or barrier semaphores. Data moves between devices by JAX's collectives and lax.ppermute only.
A program may use at most 192 MiB of HBM per device.

```python
import math
import jax
import jax.numpy as jnp
from jax import lax

B = 4
NX = 96
NY = 96
NZ = 96
ORBS = 16
N_BAND = 4


def with_ends(entries, stream_key, low, high):
    place = [jax.random.randint(jax.random.fold_in(stream_key, axis), (), 0, length) for axis, length in enumerate(entries.shape)]
    longest = entries.shape.index(max(entries.shape))
    beside = place[:longest] + [(place[longest] + 1) % entries.shape[longest]] + place[longest + 1:]
    return entries.at[tuple(place)].set(low).at[tuple(beside)].set(high)


def steps_of(key, extent, pieces, smallest, top_value):
    loudness = 1.0
    for dim, shards_of in pieces:
        steps = jax.random.uniform(jax.random.fold_in(jax.random.fold_in(key, 6), dim), (shards_of,), jnp.float32, smallest / len(pieces), top_value / len(pieces))
        loudness = loudness * jnp.repeat(jnp.exp(steps), extent[dim] // shards_of).reshape((-1,) + (1,) * (len(extent) - 1 - dim))
    return loudness


def normal_values(rng, dims, deviation, limit, pieces=(), kind=jnp.bfloat16):
    gain = steps_of(rng, dims, pieces, -0.22, 0.18) if pieces else 1.0
    drawn = jax.random.normal(rng, dims, jnp.float32) * deviation * gain
    return jnp.minimum(jnp.maximum(drawn, -limit), limit).astype(kind)


def setup_inputs(seed: int = 0) -> dict:
    key_list = jax.random.split(jax.random.key(seed), 4)
    return {
        "orbitals": normal_values(key_list[0], (ORBS, NX, NY * NZ), 1.0, 6.0, ((0, 4), (1, 8)), jnp.float32),
        "pair_mask": with_ends((jax.random.randint(key_list[1], (ORBS, B), 0, 4) < 3).astype(jnp.int32), jax.random.fold_in(key_list[1], 1), 0, 1),
        "cycle_step": jax.random.randint(key_list[2], (), 1, N_BAND).astype(jnp.int32),
    }


box_length = 16.0


def folded(index, length):
    return jnp.where(index * 2 >= length, index - length, index).astype(jnp.float32)


def reference(orbitals, pair_mask, cycle_step):
    orbit_total = orbitals.shape[0]
    fields_full = orbitals.reshape(orbit_total, NX, NY, NZ)
    freq_x = folded(jnp.arange(NX, dtype=jnp.int32), NX)
    freq_y = folded(jnp.arange(NY, dtype=jnp.int32), NY)
    freq_z = folded(jnp.arange(NZ, dtype=jnp.int32), NZ)
    squares = freq_x[:, None, None] ** 2 + freq_y[None, :, None] ** 2 + freq_z[None, None, :] ** 2
    coulomb = box_length * box_length / math.pi
    kernel = jnp.where(squares > 0.5, coulomb / jnp.maximum(squares, 1.0), jnp.float32(0.0))
    mask_float = pair_mask.astype(jnp.float32)

    def one_orbital(index):
        group = index // B
        start = (((group - cycle_step) % N_BAND) * B).astype(jnp.int32)
        visiting = lax.dynamic_slice_in_dim(fields_full, start, B, 0)
        own = lax.dynamic_index_in_dim(fields_full, index, 0, keepdims=False)
        density = own[None] * visiting
        spectra = jnp.fft.fftn(density, axes=(1, 2, 3)) * kernel
        potential = jnp.real(jnp.fft.ifftn(spectra, axes=(1, 2, 3)))
        weights = lax.dynamic_index_in_dim(mask_float, index, 0, keepdims=False)
        return -jnp.einsum('j,jxyz->xyz', weights, potential * visiting, precision=lax.Precision.HIGHEST)

    fields = lax.map(one_orbital, jnp.arange(orbit_total, dtype=jnp.int32))
    exchange_field = fields.reshape(orbit_total, NX, NY * NZ).astype(jnp.float32)
    grouped_orbs = orbitals.reshape(N_BAND, B, NX * NY * NZ)
    grouped_field = exchange_field.reshape(N_BAND, B, NX * NY * NZ)
    projection = jnp.einsum('gar,gcr->gac', grouped_orbs, grouped_field, precision=lax.Precision.HIGHEST)
    projection = (projection / (NX * NY * NZ)).reshape(orbit_total, B)
    return exchange_field, projection
```

```python
import functools
import math

import jax
import jax.numpy as jnp
import ml_dtypes
import numpy as np
from jax import lax
from jax.experimental import pallas as pl
from jax.experimental.pallas import tpu as pltpu
from jax.sharding import PartitionSpec as P

NX = 96
NY = 96
NZ = 96
LANES = 128


box_length = 16.0
highest = lax.Precision.HIGHEST


def passed_along(block, axis, distance):
    devices = range(lax.axis_size(axis))
    route = [((i - distance) % len(devices), i) for i in devices]
    return lax.ppermute(block, axis, route)


def hartley_table(length):
    index = jnp.arange(length, dtype=jnp.int32)
    product = index[:, None] * index[None, :] % length
    angle = product.astype(jnp.float32) * (2.0 * math.pi / length)
    return jnp.cos(angle) + jnp.sin(angle)


def folded(index, length):
    return jnp.where(index * 2 >= length, index - length, index).astype(jnp.float32)


def across_planes(field, table_y, table_z):
    count = field.shape[0]
    planes = field.shape[1]
    shaped = field.reshape(count * planes * NY, NZ)
    shaped = jnp.matmul(shaped, table_z, precision=highest)
    shaped = shaped.reshape(count * planes, NY, NZ)
    shaped = jnp.matmul(table_y, shaped, precision=highest)
    return shaped.reshape(count, planes, NY * NZ)


def slab_plan(orbitals, pair_mask, cycle_step):
    orbit_count = orbitals.shape[0]
    planes = orbitals.shape[1]
    grid_count = lax.axis_size("grid")
    slab_rows = NY // grid_count

    def one_hop(turn, block):
        return passed_along(block, "band", 1)

    visiting = lax.fori_loop(0, cycle_step, one_hop, orbitals)
    table_x = hartley_table(NX)
    table_y = hartley_table(NY)
    table_z = hartley_table(NZ)
    row_index = lax.axis_index("grid") * slab_rows + jnp.arange(slab_rows, dtype=jnp.int32)
    freq_x = folded(jnp.arange(NX, dtype=jnp.int32), NX)
    freq_y = folded(row_index, NY)
    freq_z = folded(jnp.arange(NZ, dtype=jnp.int32), NZ)
    squares = freq_x[:, None, None] ** 2 + freq_y[None, :, None] ** 2 + freq_z[None, None, :] ** 2
    coulomb = box_length * box_length / math.pi / (NX * NY * NZ)
    kernel = jnp.where(squares > 0.5, coulomb / jnp.maximum(squares, 1.0), jnp.float32(0.0))
    kernel = kernel.reshape(NX, slab_rows * NZ)

    def solve_items(spectra):
        along = jnp.matmul(table_x, spectra, precision=highest) * kernel
        along = jnp.matmul(table_x, along, precision=highest)
        return lax.all_to_all(along, "grid", split_axis=1, concat_axis=2, tiled=True)

    mask_float = pair_mask.astype(jnp.float32).reshape(
        orbit_count // orbit_count, orbit_count, orbit_count
    )
    own_rows = orbitals.reshape(orbit_count // orbit_count, orbit_count, planes, NY * NZ)

    def one_group(carry, inputs):
        rows, weights = inputs
        density = (rows[:, None] * visiting[None]).reshape(
            orbit_count * orbit_count, planes, NY * NZ
        )
        spectra = across_planes(density, table_y, table_z)
        potential = solve_items(
            lax.all_to_all(spectra, "grid", split_axis=2, concat_axis=1, tiled=True)
        )
        potential = across_planes(potential, table_y, table_z)
        potential = potential.reshape(orbit_count, orbit_count, planes, NY * NZ)
        field = -jnp.einsum("aj,ajxr->axr", weights, potential * visiting[None], precision=highest)
        return (carry, field)

    start_carry = jnp.zeros((), jnp.float32)
    _, fields = lax.scan(one_group, start_carry, (own_rows, mask_float))
    exchange_field = fields.reshape(orbit_count, planes, NY * NZ)
    local_terms = jnp.einsum("axr,cxr->ac", orbitals, exchange_field, precision=highest) / (
        NX * NY * NZ
    )
    projection = lax.psum(local_terms, "grid")
    return (exchange_field, projection)


SLABS = 8
GROUP = 4
SLAB_PLANES = NX // SLABS
COLS = NY * NZ // LANES
SLAB_ROWS = SLAB_PLANES * COLS
QUADS = NY // 4

bf16 = jnp.bfloat16
f32 = jnp.float32
in_vmem = pl.BlockSpec(memory_space=pltpu.VMEM)
in_smem = pl.BlockSpec(memory_space=pltpu.SMEM)
anywhere = pl.BlockSpec(memory_space=pl.ANY)


def high_low(table):
    high = table.astype(ml_dtypes.bfloat16)
    return high, (table - high.astype(np.float64)).astype(ml_dtypes.bfloat16)


def cas_table(length):
    index = np.arange(length)
    angle = (index[:, None] * index[None, :] % length) * (2.0 * np.pi / length)
    return np.cos(angle) + np.sin(angle)


def lane_table(table):
    high, low = high_low(table)
    out = np.zeros((2 * LANES, 2 * LANES), high.dtype)
    for row in (0, LANES):
        out[row : row + NZ, :NZ] = high
        out[row : row + NZ, LANES : LANES + NZ] = low
    return out


def row_table(table):
    high, low = high_low(table)
    return np.concatenate([np.concatenate([high, high], 1), np.concatenate([low, low], 1)], 0)


def plane_order(device):
    return np.concatenate([np.arange(SLAB_PLANES) + SLAB_PLANES * (device ^ k) for k in range(SLABS)])


def coulomb_table():
    index = np.arange(NY)
    freq = np.where(index * 2 >= NY, index - NY, index).astype(np.float64) ** 2
    half = np.arange(NX // 2 + 1, dtype=np.float64) ** 2
    squares = half[:, None, None] + freq[None, :, None] + freq[None, None, :]
    scale = box_length * box_length / math.pi / (NX * NY * NZ)
    out = np.zeros((NX // 2 + 1, NY, LANES), np.float32)
    out[:, :, :NZ] = np.where(squares > 0.5, scale / np.maximum(squares, 1.0), 0.0)
    return out


def split(value):
    high = value.astype(bf16)
    return high, (value - high.astype(f32)).astype(bf16)


def product(left, right):
    return lax.dot_general(left, right, (((1,), (0,)), ((), ())), preferred_element_type=f32)


def along_lanes(value, table):
    both = product(jnp.concatenate(split(value), axis=1), table)
    return both[:, :LANES] + both[:, LANES:]


def along_rows(table, value):
    both = product(table, jnp.concatenate(split(value), axis=0))
    half = both.shape[0] // 2
    return both[:half] + both[half:]


def prepare_kernel(place, block, *refs):
    outs, natural = refs[:-1], refs[-1]
    me = place[0]

    def two_columns(step, carry):
        for a in range(GROUP):
            pair = [block[:, a, pl.ds(pl.multiple_of((2 * step + i) * LANES, LANES), LANES)] for i in range(2)]
            natural[a, pl.ds(pl.multiple_of(2 * SLAB_PLANES * step, 8), 2 * SLAB_PLANES), :] = jnp.concatenate(pair, 0)
        return carry

    lax.fori_loop(0, COLS // 2, two_columns, 0, unroll=2)
    for k in range(GROUP):
        outs[k][...] = natural[(me & 3) ^ k]
        outs[GROUP + k][...] = natural[((me >> 2) * 2) ^ k]


def prepare(place, block):
    slab = jax.ShapeDtypeStruct((SLAB_ROWS, LANES), f32)
    return pl.pallas_call(
        prepare_kernel,
        out_shape=[slab] * 8,
        in_specs=[in_smem, in_vmem],
        out_specs=[in_vmem] * 8,
        scratch_shapes=[pltpu.VMEM((GROUP, SLAB_ROWS, LANES), f32)],
        compiler_params=pltpu.CompilerParams(vmem_limit_bytes=32 << 20),
        cost_estimate=pl.CostEstimate(flops=0, bytes_accessed=6 << 20, transcendentals=0),
    )(place, block)


def pair_kernel(turn, place, mask, *refs):
    own_slabs, refs = refs[:SLABS], refs[SLABS:]
    vis_slabs, refs = refs[:SLABS], refs[SLABS:]
    table_z, table_y, table_x, table_back, coulomb_hbm, *refs = refs
    if turn:
        before_hbm, *refs = refs
        outs, refs = refs[:SLABS], refs[SLABS:]
    else:
        out_hbm, *refs = refs
    raw, own, vis, spectrum, coulomb, total, in_sems, side_sems, out_sems = refs
    parts = in_sems.shape[0]
    part_rows = SLAB_ROWS // parts
    part_quads = QUADS // parts

    def arrivals(part):
        rows = pl.ds(part * part_rows, part_rows)
        return [
            pltpu.make_async_copy(slab.at[rows], raw.at[i, rows], in_sems.at[part])
            for i, slab in enumerate((*own_slabs, *vis_slabs))
        ]

    for part in range(parts):
        for copy in arrivals(part):
            copy.start()
    side = [pltpu.make_async_copy(coulomb_hbm, coulomb, side_sems.at[0])]
    if turn:
        side.append(pltpu.make_async_copy(before_hbm, total, side_sems.at[1]))
    for copy in side:
        copy.start()

    def in_order(step, first, out):
        rows = pl.ds(pl.multiple_of(2 * SLAB_PLANES * step, 8), 2 * SLAB_PLANES)
        pieces = [raw[first + k, rows, :] for k in range(SLABS)]
        out[2 * step] = jnp.concatenate([piece[:SLAB_PLANES] for piece in pieces], axis=0)
        out[2 * step + 1] = jnp.concatenate([piece[SLAB_PLANES:] for piece in pieces], axis=0)

    def lane_index():
        return lax.broadcasted_iota(jnp.int32, (NX, LANES), 1)

    def forward(quad, carry):
        lane = lane_index()
        first, second, third = [own[3 * quad + i] * vis[3 * quad + i] for i in range(3)]
        rows = [
            first,
            pltpu.roll(jnp.where(lane >= 96, first, second), 32, 1),
            pltpu.roll(jnp.where(lane >= 64, second, third), 64, 1),
            pltpu.roll(third, 96, 1),
        ]
        done = along_lanes(jnp.concatenate(rows, axis=0), table_z[...])
        for j in range(2):
            both = jnp.concatenate([done[2 * j * NX : (2 * j + 1) * NX], done[(2 * j + 1) * NX : (2 * j + 2) * NX]], 1)
            both = along_rows(table_x[...], both)
            spectrum[4 * quad + 2 * j] = both[:, :LANES]
            spectrum[4 * quad + 2 * j + 1] = both[:, LANES:]
        return carry

    for part in range(parts):
        for copy in arrivals(part):
            copy.wait()

        def relay(step, carry):
            in_order(step, 0, own)
            in_order(step, SLABS, vis)
            return carry

        lax.fori_loop(part * part_quads * 3 // 2, (part + 1) * part_quads * 3 // 2, relay, 0)
        lax.fori_loop(part * part_quads, (part + 1) * part_quads, forward, 0, unroll=min(4, part_quads))
    for copy in side:
        copy.wait()

    def middle(step, carry):
        base = pl.multiple_of(8 * step, 8)
        block = jnp.swapaxes(spectrum[:, pl.ds(base, 8), :], 0, 1)
        rows = []
        for j in range(4):
            both = along_rows(table_y[...], jnp.concatenate([block[2 * j], block[2 * j + 1]], axis=1))
            at = [base + 2 * j, base + 2 * j + 1]
            both = both * jnp.concatenate([coulomb[jnp.minimum(i, NX - i)] for i in at], axis=1)
            both = along_rows(table_y[...], both)
            rows += [both[:, :LANES], both[:, LANES:]]
        spectrum[:, pl.ds(base, 8), :] = jnp.swapaxes(jnp.stack(rows, axis=0), 0, 1)
        return carry

    lax.fori_loop(0, NX // 8, middle, 0, unroll=2)
    me = place[0]
    weight = -mask[me & 3, (me >> 2) * 2 + turn].astype(f32)

    def back(quad, carry):
        lane = lane_index()
        rows = []
        for j in range(2):
            both = jnp.concatenate([spectrum[4 * quad + 2 * j], spectrum[4 * quad + 2 * j + 1]], axis=1)
            both = along_rows(table_back[...], both)
            rows += [both[:, :LANES], both[:, LANES:]]
        done = along_lanes(jnp.concatenate(rows, axis=0), table_z[...])
        first, second, third, fourth = [done[NX * i : NX * (i + 1)] for i in range(4)]
        second = pltpu.roll(second, 96, 1)
        third = pltpu.roll(third, 64, 1)
        fourth = pltpu.roll(fourth, 32, 1)
        columns = (
            jnp.where(lane < 96, first, second),
            jnp.where(lane < 64, second, third),
            jnp.where(lane < 32, third, fourth),
        )
        for i in range(3):
            value = weight * (columns[i] * vis[3 * quad + i])
            if turn:
                value = total[3 * quad + i] + value
            total[3 * quad + i] = value
        return carry

    leaving = []
    for part in range(parts):
        lax.fori_loop(part * part_quads, (part + 1) * part_quads, back, 0, unroll=min(4, part_quads))
        if turn:

            def apart(step, carry):
                rows = pl.ds(pl.multiple_of(2 * SLAB_PLANES * step, 8), 2 * SLAB_PLANES)
                even, odd = total[2 * step], total[2 * step + 1]
                for k in range(SLABS):
                    cut = slice(SLAB_PLANES * k, SLAB_PLANES * (k + 1))
                    raw[k, rows, :] = jnp.concatenate([even[cut], odd[cut]], axis=0)
                return carry

            lax.fori_loop(part * part_quads * 3 // 2, (part + 1) * part_quads * 3 // 2, apart, 0)
            rows = pl.ds(part * part_rows, part_rows)
            copies = [pltpu.make_async_copy(raw.at[k, rows], outs[k].at[rows], out_sems.at[part]) for k in range(SLABS)]
        else:
            cols = pl.ds(part * part_quads * 3, part_quads * 3)
            copies = [pltpu.make_async_copy(total.at[cols], out_hbm.at[cols], out_sems.at[part])]
        for copy in copies:
            copy.start()
        leaving += copies
    for copy in leaving:
        copy.wait()


def pair_step(turn, place, mask, own_slabs, vis_slabs, tables, before=None):
    parts = 4
    extra = [] if before is None else [before]
    whole = jax.ShapeDtypeStruct((COLS, NX, LANES), f32)
    slab = jax.ShapeDtypeStruct((SLAB_ROWS, LANES), f32)
    return pl.pallas_call(
        functools.partial(pair_kernel, turn),
        out_shape=[slab] * SLABS if turn else whole,
        in_specs=[in_smem] * 2 + [anywhere] * (2 * SLABS) + [in_vmem] * 4 + [anywhere] * (1 + len(extra)),
        out_specs=[anywhere] * SLABS if turn else anywhere,
        scratch_shapes=[
            pltpu.VMEM((2 * SLABS, SLAB_ROWS, LANES), f32),
            pltpu.VMEM((COLS, NX, LANES), f32),
            pltpu.VMEM((COLS, NX, LANES), f32),
            pltpu.VMEM((NY, NX, LANES), f32),
            pltpu.VMEM((NX // 2 + 1, NY, LANES), f32),
            pltpu.VMEM((COLS, NX, LANES), f32),
            pltpu.SemaphoreType.DMA((parts,)),
            pltpu.SemaphoreType.DMA((2,)),
            pltpu.SemaphoreType.DMA((parts,)),
        ],
        compiler_params=pltpu.CompilerParams(vmem_limit_bytes=40 << 20),
        cost_estimate=pl.CostEstimate(flops=16 * 10**9, bytes_accessed=16 << 20, transcendentals=0),
    )(place, mask, *own_slabs, *vis_slabs, *tables, *extra)


def finish_kernel(place, *refs):
    parts, refs = refs[:SLABS], refs[SLABS:]
    own, refs = refs[:GROUP], refs[GROUP:]
    out, gram, natural = refs
    me = place[0] & 3
    for k in range(GROUP):
        natural[me ^ k] = parts[k][...] + parts[k + GROUP][...]
    sums = []
    for a in range(GROUP):
        for c in range(GROUP):
            terms = own[a][...] * natural[me ^ c]
            terms = jnp.sum(terms.reshape(SLAB_ROWS // 8, 8, LANES), axis=0)
            sums.append(jnp.sum(terms, axis=0, keepdims=True))
    gram[...] = jnp.concatenate(sums, axis=0)

    def two_columns(step, carry):
        rows = pl.ds(pl.multiple_of(2 * SLAB_PLANES * step, 8), 2 * SLAB_PLANES)
        for a in range(GROUP):
            pair = natural[a, rows, :]
            for i in range(2):
                lanes = pl.ds(pl.multiple_of((2 * step + i) * LANES, LANES), LANES)
                out[:, a, lanes] = pair[SLAB_PLANES * i : SLAB_PLANES * (i + 1)]
        return carry

    lax.fori_loop(0, COLS // 2, two_columns, 0, unroll=2)


def finish(place, parts, own):
    return pl.pallas_call(
        finish_kernel,
        out_shape=[
            jax.ShapeDtypeStruct((SLAB_PLANES, GROUP, NY * NZ), f32),
            jax.ShapeDtypeStruct((GROUP * GROUP, LANES), f32),
        ],
        in_specs=[in_smem] + [in_vmem] * (SLABS + GROUP),
        out_specs=[in_vmem] * 2,
        scratch_shapes=[pltpu.VMEM((GROUP, SLAB_ROWS, LANES), f32)],
        compiler_params=pltpu.CompilerParams(vmem_limit_bytes=32 << 20),
        cost_estimate=pl.CostEstimate(flops=0, bytes_accessed=8 << 20, transcendentals=0),
    )(place, *parts, *own)


def to_partner(block, flip):
    return lax.ppermute(block, "grid", [(i, i ^ flip) for i in range(SLABS)])


def to_group(block, distance, flip):
    bands = lax.axis_size("band")
    route = [(b * SLABS + i, (b + distance) % bands * SLABS + (i ^ flip)) for b in range(bands) for i in range(SLABS)]
    return lax.ppermute(block, ("band", "grid"), route)


def pair_plan(orbitals, pair_mask, cycle_step):
    me = lax.axis_index("grid")
    place = me.astype(jnp.int32).reshape(1)
    cas = cas_table(NX)
    forward_x = np.stack([row_table(cas[:, plane_order(d)]) for d in range(SLABS)])
    back_x = np.stack([row_table(cas[plane_order(d), :]) for d in range(SLABS)])
    tables = (
        jnp.asarray(lane_table(cas)),
        jnp.asarray(row_table(cas)),
        lax.dynamic_index_in_dim(jnp.asarray(forward_x), me, keepdims=False),
        lax.dynamic_index_in_dim(jnp.asarray(back_x), me, keepdims=False),
        jnp.asarray(coulomb_table()),
    )
    slabs = prepare(place, jnp.transpose(orbitals, (1, 0, 2)))

    def with_distance(distance, slabs, pair_mask, place, tables):
        own_out, vis_out = slabs[:GROUP], slabs[GROUP:]
        vis = [[to_group(vis_out[t], distance, 0), to_group(vis_out[2 + t], distance, 4)] for t in range(2)]
        own = [own_out[0]] + [to_partner(own_out[k], k) for k in range(1, GROUP)]
        own += [to_partner(own[k], 4) for k in range(GROUP)]
        visiting = []
        for t in range(2):
            home, across = vis[t]
            beside, diagonal = to_partner(home, 2), to_partner(across, 2)
            cored = [to_partner(slab, 1) for slab in (home, beside, across, diagonal)]
            visiting.append([home, cored[0], beside, cored[1], across, cored[2], diagonal, cored[3]])
        total = pair_step(0, place, pair_mask, own, visiting[0], tables)
        parts = pair_step(1, place, pair_mask, own, visiting[1], tables, total)
        parts = [parts[0]] + [to_partner(parts[k], k) for k in range(1, SLABS)]
        return finish(place, parts, own_out)

    bands = lax.axis_size("band")
    field, gram = lax.switch(
        cycle_step - 1,
        [functools.partial(with_distance, distance) for distance in range(1, bands)],
        slabs,
        pair_mask,
        place,
        tables,
    )
    gram = jnp.sum(gram, axis=1).reshape(GROUP, GROUP) / (NX * NY * NZ)
    order = (me & 3) ^ jnp.arange(GROUP, dtype=jnp.int32)
    gram = jnp.take(jnp.take(gram, order, axis=0), order, axis=1)
    return jnp.transpose(field, (1, 0, 2)), lax.psum(gram, "grid")


def shards(orbitals, pair_mask, cycle_step):
    if lax.axis_size("grid") == SLABS and orbitals.shape[0] == GROUP:
        return pair_plan(orbitals, pair_mask, cycle_step)
    return slab_plan(orbitals, pair_mask, cycle_step)


def solution(mesh):
    return jax.shard_map(
        shards,
        mesh=mesh,
        in_specs=(P("band", "grid", None), P("band", None), P()),
        out_specs=(P("band", "grid", None), P("band", None)),
        check_vma=False,
    )
```

```python
import functools
import math

import jax
import jax.numpy as jnp
import ml_dtypes
import numpy as np
from jax import lax
from jax.experimental import pallas as pl
from jax.experimental.pallas import tpu as pltpu
from jax.sharding import PartitionSpec as P

NX = 96
NY = 96
NZ = 96
LANES = 128


box_length = 16.0
highest = lax.Precision.HIGHEST


def passed_along(block, axis, distance):
    devices = range(lax.axis_size(axis))
    route = [((i - distance) % len(devices), i) for i in devices]
    return lax.ppermute(block, axis, route)


def hartley_table(length):
    index = jnp.arange(length, dtype=jnp.int32)
    product = index[:, None] * index[None, :] % length
    angle = product.astype(jnp.float32) * (2.0 * math.pi / length)
    return jnp.cos(angle) + jnp.sin(angle)


def folded(index, length):
    return jnp.where(index * 2 >= length, index - length, index).astype(jnp.float32)


def across_planes(field, table_y, table_z):
    count = field.shape[0]
    planes = field.shape[1]
    shaped = field.reshape(count * planes * NY, NZ)
    shaped = jnp.matmul(shaped, table_z, precision=highest)
    shaped = shaped.reshape(count * planes, NY, NZ)
    shaped = jnp.matmul(table_y, shaped, precision=highest)
    return shaped.reshape(count, planes, NY * NZ)


def slab_plan(orbitals, pair_mask, cycle_step):
    orbit_count = orbitals.shape[0]
    planes = orbitals.shape[1]
    grid_count = lax.axis_size("grid")
    slab_rows = NY // grid_count

    def one_hop(turn, block):
        return passed_along(block, "band", 1)

    visiting = lax.fori_loop(0, cycle_step, one_hop, orbitals)
    table_x = hartley_table(NX)
    table_y = hartley_table(NY)
    table_z = hartley_table(NZ)
    row_index = lax.axis_index("grid") * slab_rows + jnp.arange(slab_rows, dtype=jnp.int32)
    freq_x = folded(jnp.arange(NX, dtype=jnp.int32), NX)
    freq_y = folded(row_index, NY)
    freq_z = folded(jnp.arange(NZ, dtype=jnp.int32), NZ)
    squares = freq_x[:, None, None] ** 2 + freq_y[None, :, None] ** 2 + freq_z[None, None, :] ** 2
    coulomb = box_length * box_length / math.pi / (NX * NY * NZ)
    kernel = jnp.where(squares > 0.5, coulomb / jnp.maximum(squares, 1.0), jnp.float32(0.0))
    kernel = kernel.reshape(NX, slab_rows * NZ)

    def solve_items(spectra):
        along = jnp.matmul(table_x, spectra, precision=highest) * kernel
        along = jnp.matmul(table_x, along, precision=highest)
        return lax.all_to_all(along, "grid", split_axis=1, concat_axis=2, tiled=True)

    mask_float = pair_mask.astype(jnp.float32).reshape(
        orbit_count // orbit_count, orbit_count, orbit_count
    )
    own_rows = orbitals.reshape(orbit_count // orbit_count, orbit_count, planes, NY * NZ)

    def one_group(carry, inputs):
        rows, weights = inputs
        density = (rows[:, None] * visiting[None]).reshape(
            orbit_count * orbit_count, planes, NY * NZ
        )
        spectra = across_planes(density, table_y, table_z)
        potential = solve_items(
            lax.all_to_all(spectra, "grid", split_axis=2, concat_axis=1, tiled=True)
        )
        potential = across_planes(potential, table_y, table_z)
        potential = potential.reshape(orbit_count, orbit_count, planes, NY * NZ)
        field = -jnp.einsum("aj,ajxr->axr", weights, potential * visiting[None], precision=highest)
        return (carry, field)

    start_carry = jnp.zeros((), jnp.float32)
    _, fields = lax.scan(one_group, start_carry, (own_rows, mask_float))
    exchange_field = fields.reshape(orbit_count, planes, NY * NZ)
    local_terms = jnp.einsum("axr,cxr->ac", orbitals, exchange_field, precision=highest) / (
        NX * NY * NZ
    )
    projection = lax.psum(local_terms, "grid")
    return (exchange_field, projection)


SLABS = 8
GROUP = 4
SLAB_PLANES = NX // SLABS
COLS = NY * NZ // LANES
SLAB_ROWS = SLAB_PLANES * COLS
OCTETS = NY // 8
UNROLL = (4, 4, 4)
PAIR_VMEM = 36 << 20

bf16 = jnp.bfloat16
f32 = jnp.float32
in_vmem = pl.BlockSpec(memory_space=pltpu.VMEM)
in_smem = pl.BlockSpec(memory_space=pltpu.SMEM)


def high_low(table):
    high = table.astype(ml_dtypes.bfloat16)
    return high, (table - high.astype(np.float64)).astype(ml_dtypes.bfloat16)


def cas_table(length):
    index = np.arange(length)
    angle = (index[:, None] * index[None, :] % length) * (2.0 * np.pi / length)
    return np.cos(angle) + np.sin(angle)


def lane_table(table):
    high, low = high_low(table)
    out = np.zeros((2 * LANES, 2 * LANES), high.dtype)
    for row in (0, LANES):
        out[row : row + NZ, :NZ] = high
        out[row : row + NZ, LANES : LANES + NZ] = low
    return out


def row_table(table):
    high, low = high_low(table)
    return np.concatenate([np.concatenate([high, high], 1), np.concatenate([low, low], 1)], 0)


def plane_order(device):
    return np.concatenate([np.arange(SLAB_PLANES) + SLAB_PLANES * (device ^ k) for k in range(SLABS)])


def split(value):
    high = value.astype(bf16)
    return high, (value - high.astype(f32)).astype(bf16)


def product(left, right):
    return lax.dot_general(left, right, (((1,), (0,)), ((), ())), preferred_element_type=f32)


def along_lanes(value, table):
    both = product(jnp.concatenate(split(value), axis=1), table)
    return both[:, :LANES] + both[:, LANES:]


def along_rows(table, value):
    both = product(table, jnp.concatenate(split(value), axis=0))
    half = both.shape[0] // 2
    return both[:half] + both[half:]


def prepare_kernel(place, block, *refs):
    outs, natural = refs[:-1], refs[-1]
    me = place[0]

    def two_columns(step, carry):
        for a in range(GROUP):
            pair = [block[:, a, pl.ds(pl.multiple_of((2 * step + i) * LANES, LANES), LANES)] for i in range(2)]
            natural[a, pl.ds(pl.multiple_of(2 * SLAB_PLANES * step, 8), 2 * SLAB_PLANES), :] = jnp.concatenate(pair, 0)
        return carry

    lax.fori_loop(0, COLS // 2, two_columns, 0, unroll=2)
    for k in range(GROUP):
        outs[min(k, 2)][k // 3] = natural[(me & 3) ^ k]
        outs[3 + k][0] = natural[((me >> 2) * 2) ^ k]


def prepare(place, block):
    slabs = [jax.ShapeDtypeStruct((count, SLAB_ROWS, LANES), f32) for count in (1, 1, 2, 1, 1, 1, 1)]
    return pl.pallas_call(
        prepare_kernel,
        out_shape=slabs,
        in_specs=[in_smem, in_vmem],
        out_specs=[in_vmem] * 7,
        scratch_shapes=[pltpu.VMEM((GROUP, SLAB_ROWS, LANES), f32)],
        compiler_params=pltpu.CompilerParams(vmem_limit_bytes=32 << 20),
        cost_estimate=pl.CostEstimate(flops=0, bytes_accessed=6 << 20, transcendentals=0),
    )(place, block)


def tables_kernel(place, lanes_in, rows_in, forward_in, back_in, table_z, table_y, table_x, table_back, coulomb, sems):
    me = place[0]
    copies = [
        pltpu.make_async_copy(source, target, sems.at[i])
        for i, (source, target) in enumerate(
            ((lanes_in, table_z), (rows_in, table_y), (forward_in.at[me], table_x), (back_in.at[me], table_back))
        )
    ]
    for copy in copies:
        copy.start()
    scale = box_length * box_length / math.pi / (NX * NY * NZ)
    row = lax.broadcasted_iota(jnp.int32, (NY, LANES), 0)
    lane = lax.broadcasted_iota(jnp.int32, (NY, LANES), 1)
    plane = jnp.minimum(row, NY - row) ** 2 + jnp.minimum(lane, NZ - lane) ** 2
    plane = plane.astype(f32)

    def one_plane(x, carry):
        squares = plane + (x * x).astype(f32)
        coulomb[x] = jnp.where((squares > 0.5) & (lane < NZ), scale / jnp.maximum(squares, 1.0), 0.0)
        return carry

    lax.fori_loop(0, NX // 2 + 1, one_plane, 0)
    for copy in copies:
        copy.wait()


def make_tables(place, tables):
    return pl.pallas_call(
        tables_kernel,
        out_shape=[
            jax.ShapeDtypeStruct(tables[0].shape, bf16),
            *[jax.ShapeDtypeStruct(tables[1].shape, bf16)] * 3,
            jax.ShapeDtypeStruct((NX // 2 + 1, NY, LANES), f32),
        ],
        in_specs=[in_smem] + [pl.BlockSpec(memory_space=pl.ANY)] * 4,
        out_specs=[in_vmem] * 5,
        scratch_shapes=[pltpu.SemaphoreType.DMA((4,))],
        compiler_params=pltpu.CompilerParams(vmem_limit_bytes=16 << 20),
        cost_estimate=pl.CostEstimate(flops=0, bytes_accessed=1 << 20, transcendentals=0),
    )(place, *tables)


OWN_PLACES = ((0, 0), (1, 0), (2, 0), (3, 1), (4, 0), (5, 0), (6, 0), (7, 1))
VISITING_PLACES = (
    ((0, 0), (1, 0), (2, 0), (3, 0), (0, 1), (1, 1), (2, 1), (3, 1)),
    tuple((k, 0) for k in range(SLABS)),
)


def pair_kernel(turn, place, mask, *refs):
    places = VISITING_PLACES[turn]
    count = 1 + max(i for i, _ in places)
    own_refs, vis_refs, refs = refs[:SLABS], refs[SLABS : SLABS + count], refs[SLABS + count :]
    own_slabs = [own_refs[i].at[j] for i, j in OWN_PLACES]
    vis_slabs = [vis_refs[i].at[j] for i, j in places]
    table_z, table_y, table_x, table_back, coulomb, *refs = refs
    if turn:
        before, *refs = refs
        outs, refs = refs[:SLABS], refs[SLABS:]
    else:
        out, *refs = refs
    vis, spectrum = refs
    me = place[0]
    weight = -mask[me & 3, (me >> 2) * 2 + turn].astype(f32)

    def rows_of(step):
        return pl.ds(pl.multiple_of(2 * SLAB_PLANES * step, 8), 2 * SLAB_PLANES)

    def columns_of(slabs, step):
        pieces = [slab[rows_of(step), :] for slab in slabs]
        return [
            jnp.concatenate([piece[:SLAB_PLANES] for piece in pieces], axis=0),
            jnp.concatenate([piece[SLAB_PLANES:] for piece in pieces], axis=0),
        ]

    def lane_index():
        return lax.broadcasted_iota(jnp.int32, (NX, LANES), 1)

    def forward(octet, carry):
        lane = lane_index()
        densities = []
        for i in range(3):
            step = 3 * octet + i
            pair = columns_of(vis_slabs, step)
            for j in range(2):
                vis[2 * step + j] = pair[j]
            densities += [a * b for a, b in zip(columns_of(own_slabs, step), pair)]
        for q in range(2):
            first, second, third = densities[3 * q : 3 * q + 3]
            rows = [
                first,
                pltpu.roll(jnp.where(lane >= 96, first, second), 32, 1),
                pltpu.roll(jnp.where(lane >= 64, second, third), 64, 1),
                pltpu.roll(third, 96, 1),
            ]
            done = along_lanes(jnp.concatenate(rows, axis=0), table_z[...])
            for j in range(2):
                both = [done[(2 * j + i) * NX : (2 * j + i + 1) * NX] for i in range(2)]
                both = along_rows(table_x[...], jnp.concatenate(both, axis=1))
                at = 8 * octet + 4 * q + 2 * j
                spectrum[at] = both[:, :LANES]
                spectrum[at + 1] = both[:, LANES:]
        return carry

    lax.fori_loop(0, OCTETS, forward, 0, unroll=UNROLL[0])

    def middle(step, carry):
        base = pl.multiple_of(8 * step, 8)
        block = jnp.swapaxes(spectrum[:, pl.ds(base, 8), :], 0, 1)
        rows = []
        for j in range(4):
            both = along_rows(table_y[...], jnp.concatenate([block[2 * j], block[2 * j + 1]], axis=1))
            at = [base + 2 * j, base + 2 * j + 1]
            both = both * jnp.concatenate([coulomb[jnp.minimum(i, NX - i)] for i in at], axis=1)
            both = along_rows(table_y[...], both)
            rows += [both[:, :LANES], both[:, LANES:]]
        spectrum[:, pl.ds(base, 8), :] = jnp.swapaxes(jnp.stack(rows, axis=0), 0, 1)
        return carry

    lax.fori_loop(0, NX // 8, middle, 0, unroll=UNROLL[1])

    def back(octet, carry):
        lane = lane_index()
        values = []
        for q in range(2):
            rows = []
            for j in range(2):
                at = 8 * octet + 4 * q + 2 * j
                both = along_rows(table_back[...], jnp.concatenate([spectrum[at], spectrum[at + 1]], axis=1))
                rows += [both[:, :LANES], both[:, LANES:]]
            done = along_lanes(jnp.concatenate(rows, axis=0), table_z[...])
            first, second, third, fourth = [done[NX * i : NX * (i + 1)] for i in range(4)]
            second = pltpu.roll(second, 96, 1)
            third = pltpu.roll(third, 64, 1)
            fourth = pltpu.roll(fourth, 32, 1)
            columns = (
                jnp.where(lane < 96, first, second),
                jnp.where(lane < 64, second, third),
                jnp.where(lane < 32, third, fourth),
            )
            for i in range(3):
                at = 6 * octet + 3 * q + i
                value = weight * (columns[i] * vis[at])
                if turn:
                    values.append(before[at] + value)
                else:
                    out[at] = value
        if turn:
            for i in range(3):
                even, odd = values[2 * i : 2 * i + 2]
                for k in range(SLABS):
                    cut = slice(SLAB_PLANES * k, SLAB_PLANES * (k + 1))
                    outs[k][rows_of(3 * octet + i), :] = jnp.concatenate([even[cut], odd[cut]], axis=0)
        return carry

    lax.fori_loop(0, OCTETS, back, 0, unroll=UNROLL[2])


def pair_step(turn, place, mask, own, visiting, tables, before=None):
    extra = [] if before is None else [before]
    whole = jax.ShapeDtypeStruct((COLS, NX, LANES), f32)
    slab = jax.ShapeDtypeStruct((SLAB_ROWS, LANES), f32)
    return pl.pallas_call(
        functools.partial(pair_kernel, turn),
        out_shape=[slab] * SLABS if turn else whole,
        in_specs=[in_smem] * 2 + [in_vmem] * (len(own) + len(visiting) + 5 + len(extra)),
        out_specs=[in_vmem] * SLABS if turn else in_vmem,
        scratch_shapes=[
            pltpu.VMEM((COLS, NX, LANES), f32),
            pltpu.VMEM((NY, NX, LANES), f32),
        ],
        compiler_params=pltpu.CompilerParams(vmem_limit_bytes=PAIR_VMEM),
        cost_estimate=pl.CostEstimate(flops=0, bytes_accessed=1 << 20, transcendentals=0),
    )(place, mask, *own, *visiting, *tables, *extra)


def gram_kernel(place, *refs):
    parts, refs = refs[:SLABS], refs[SLABS:]
    own, refs = refs[:3], refs[3:]
    natural, gram = refs
    me = place[0] & 3
    for k in range(GROUP):
        natural[me ^ k] = parts[k][...] + parts[k + GROUP][...]
    for a in range(GROUP):
        for c in range(GROUP):
            terms = own[min(a, 2)][a // 3] * natural[me ^ c]
            terms = jnp.sum(terms.reshape(SLAB_ROWS // 8, 8, LANES), axis=0)
            gram[(me ^ a) * GROUP + (me ^ c)] = jnp.sum(terms, axis=0, keepdims=True)


def layout_kernel(natural, out):
    def two_columns(step, carry):
        rows = pl.ds(pl.multiple_of(2 * SLAB_PLANES * step, 8), 2 * SLAB_PLANES)
        for a in range(GROUP):
            pair = natural[a, rows, :]
            for i in range(2):
                lanes = pl.ds(pl.multiple_of((2 * step + i) * LANES, LANES), LANES)
                out[:, a, lanes] = pair[SLAB_PLANES * i : SLAB_PLANES * (i + 1)]
        return carry

    lax.fori_loop(0, COLS // 2, two_columns, 0, unroll=2)


def finish(place, parts, own):
    natural, gram = pl.pallas_call(
        gram_kernel,
        out_shape=[
            jax.ShapeDtypeStruct((GROUP, SLAB_ROWS, LANES), f32),
            jax.ShapeDtypeStruct((GROUP * GROUP, 1, LANES), f32),
        ],
        in_specs=[in_smem] + [in_vmem] * (SLABS + 3),
        out_specs=[in_vmem] * 2,
        compiler_params=pltpu.CompilerParams(vmem_limit_bytes=32 << 20),
        cost_estimate=pl.CostEstimate(flops=0, bytes_accessed=8 << 20, transcendentals=0),
    )(place, *parts, *own)
    field = pl.pallas_call(
        layout_kernel,
        out_shape=jax.ShapeDtypeStruct((SLAB_PLANES, GROUP, NY * NZ), f32),
        in_specs=[in_vmem],
        out_specs=in_vmem,
        compiler_params=pltpu.CompilerParams(vmem_limit_bytes=32 << 20),
        cost_estimate=pl.CostEstimate(flops=0, bytes_accessed=8 << 20, transcendentals=0),
    )(natural)
    gram = jnp.sum(gram.reshape(GROUP, GROUP, LANES), axis=2) / (NX * NY * NZ)
    for flip in (1, 2, 4):
        gram = gram + to_partner(gram, flip)
    return field, gram


def to_partner(block, flip):
    return lax.ppermute(block, "grid", [(i, i ^ flip) for i in range(SLABS)])


def to_group(block, distance, flip):
    bands = lax.axis_size("band")
    route = [(b * SLABS + i, (b + distance) % bands * SLABS + (i ^ flip)) for b in range(bands) for i in range(SLABS)]
    return lax.ppermute(block, ("band", "grid"), route)


def after(value, *others):
    return lax.optimization_barrier((value, *others))[0]


def pair_plan(orbitals, pair_mask, cycle_step):
    me = lax.axis_index("grid")
    place = me.astype(jnp.int32).reshape(1)
    cas = cas_table(NX)
    forward_x = jnp.asarray(np.stack([row_table(cas[:, plane_order(d)]) for d in range(SLABS)]))
    back_x = jnp.asarray(np.stack([row_table(cas[plane_order(d), :]) for d in range(SLABS)]))
    fixed = jnp.asarray(lane_table(cas)), jnp.asarray(row_table(cas)), forward_x, back_x
    slabs = prepare(place, jnp.transpose(orbitals, (1, 0, 2)))

    def with_distance(distance, slabs, pair_mask, place, fixed):
        own_out, vis_out = slabs[:3], slabs[3:]
        home = to_group(vis_out[0], distance, 0)
        across = to_group(vis_out[2], distance, 4)
        own_y = to_partner(own_out[0], 4)
        own_x = to_partner(own_out[2], 2)
        own_next = to_partner(own_out[1], 4)
        first = jnp.concatenate([after(home, own_x, own_y), across])
        first_x = to_partner(first, 2)
        home = to_group(after(vis_out[1], first), distance, 0)
        across = to_group(after(vis_out[3], first), distance, 4)
        tables = make_tables(after(place, first), fixed)
        own_far = to_partner(after(own_x, across, own_next, *tables), 4)
        home_x, across_x = to_partner(home, 2), to_partner(across, 2)
        cores = [to_partner(after(array, home), 1) for array in (own_out[1], own_x, own_next)]
        cores.append(to_partner(after(own_far, home_x), 1))
        own = [own_out[0], cores[0], own_x, cores[1], own_y, cores[2], own_far, cores[3]]
        visiting = [first, to_partner(after(first, home), 1), first_x, to_partner(after(first_x, home), 1)]
        total = pair_step(0, place, pair_mask, own, visiting, tables)
        cores = [to_partner(slab, 1) for slab in (home, home_x, across)]
        cores.append(to_partner(after(across_x, total), 1))
        visiting = [home, cores[0], home_x, cores[1], across, cores[2], across_x, cores[3]]
        parts = pair_step(1, place, pair_mask, own, visiting, tables, total)
        parts = [parts[0]] + [to_partner(parts[k], k) for k in range(1, SLABS)]
        return finish(place, parts, own_out)

    bands = lax.axis_size("band")
    field, gram = lax.switch(
        cycle_step - 1,
        [functools.partial(with_distance, distance) for distance in range(1, bands)],
        slabs,
        pair_mask,
        place,
        fixed,
    )
    return jnp.transpose(field, (1, 0, 2)), gram


def shards(orbitals, pair_mask, cycle_step):
    if lax.axis_size("grid") == SLABS and orbitals.shape[0] == GROUP:
        return pair_plan(orbitals, pair_mask, cycle_step)
    return slab_plan(orbitals, pair_mask, cycle_step)


def solution(mesh):
    return jax.shard_map(
        shards,
        mesh=mesh,
        in_specs=(P("band", "grid", None), P("band", None), P()),
        out_specs=(P("band", "grid", None), P("band", None)),
        check_vma=False,
    )
```

```python
import functools
import math

import jax
import jax.numpy as jnp
import ml_dtypes
import numpy as np
from jax import lax
from jax.experimental import pallas as pl
from jax.experimental.pallas import tpu as pltpu
from jax.sharding import PartitionSpec as P

NX = 96
NY = 96
NZ = 96
LANES = 128


box_length = 16.0
highest = lax.Precision.HIGHEST


def passed_along(block, axis, distance):
    devices = range(lax.axis_size(axis))
    route = [((i - distance) % len(devices), i) for i in devices]
    return lax.ppermute(block, axis, route)


def hartley_table(length):
    index = jnp.arange(length, dtype=jnp.int32)
    product = index[:, None] * index[None, :] % length
    angle = product.astype(jnp.float32) * (2.0 * math.pi / length)
    return jnp.cos(angle) + jnp.sin(angle)


def folded(index, length):
    return jnp.where(index * 2 >= length, index - length, index).astype(jnp.float32)


def across_planes(field, table_y, table_z):
    count = field.shape[0]
    planes = field.shape[1]
    shaped = field.reshape(count * planes * NY, NZ)
    shaped = jnp.matmul(shaped, table_z, precision=highest)
    shaped = shaped.reshape(count * planes, NY, NZ)
    shaped = jnp.matmul(table_y, shaped, precision=highest)
    return shaped.reshape(count, planes, NY * NZ)


def slab_plan(orbitals, pair_mask, cycle_step):
    orbit_count = orbitals.shape[0]
    planes = orbitals.shape[1]
    grid_count = lax.axis_size("grid")
    slab_rows = NY // grid_count

    def one_hop(turn, block):
        return passed_along(block, "band", 1)

    visiting = lax.fori_loop(0, cycle_step, one_hop, orbitals)
    table_x = hartley_table(NX)
    table_y = hartley_table(NY)
    table_z = hartley_table(NZ)
    row_index = lax.axis_index("grid") * slab_rows + jnp.arange(slab_rows, dtype=jnp.int32)
    freq_x = folded(jnp.arange(NX, dtype=jnp.int32), NX)
    freq_y = folded(row_index, NY)
    freq_z = folded(jnp.arange(NZ, dtype=jnp.int32), NZ)
    squares = freq_x[:, None, None] ** 2 + freq_y[None, :, None] ** 2 + freq_z[None, None, :] ** 2
    coulomb = box_length * box_length / math.pi / (NX * NY * NZ)
    kernel = jnp.where(squares > 0.5, coulomb / jnp.maximum(squares, 1.0), jnp.float32(0.0))
    kernel = kernel.reshape(NX, slab_rows * NZ)

    def solve_items(spectra):
        along = jnp.matmul(table_x, spectra, precision=highest) * kernel
        along = jnp.matmul(table_x, along, precision=highest)
        return lax.all_to_all(along, "grid", split_axis=1, concat_axis=2, tiled=True)

    mask_float = pair_mask.astype(jnp.float32).reshape(
        orbit_count // orbit_count, orbit_count, orbit_count
    )
    own_rows = orbitals.reshape(orbit_count // orbit_count, orbit_count, planes, NY * NZ)

    def one_group(carry, inputs):
        rows, weights = inputs
        density = (rows[:, None] * visiting[None]).reshape(
            orbit_count * orbit_count, planes, NY * NZ
        )
        spectra = across_planes(density, table_y, table_z)
        potential = solve_items(
            lax.all_to_all(spectra, "grid", split_axis=2, concat_axis=1, tiled=True)
        )
        potential = across_planes(potential, table_y, table_z)
        potential = potential.reshape(orbit_count, orbit_count, planes, NY * NZ)
        field = -jnp.einsum("aj,ajxr->axr", weights, potential * visiting[None], precision=highest)
        return (carry, field)

    start_carry = jnp.zeros((), jnp.float32)
    _, fields = lax.scan(one_group, start_carry, (own_rows, mask_float))
    exchange_field = fields.reshape(orbit_count, planes, NY * NZ)
    local_terms = jnp.einsum("axr,cxr->ac", orbitals, exchange_field, precision=highest) / (
        NX * NY * NZ
    )
    projection = lax.psum(local_terms, "grid")
    return (exchange_field, projection)


SLABS = 8
GROUP = 4
SLAB_PLANES = NX // SLABS
COLS = NY * NZ // LANES
SLAB_ROWS = SLAB_PLANES * COLS
OCTETS = NY // 8
PITCH = NX + 8
UNROLL = (4, 4, 4)
PAIR_VMEM = 36 << 20

bf16 = jnp.bfloat16
f32 = jnp.float32
in_vmem = pl.BlockSpec(memory_space=pltpu.VMEM)
in_smem = pl.BlockSpec(memory_space=pltpu.SMEM)


def high_low(table):
    high = table.astype(ml_dtypes.bfloat16)
    return high, (table - high.astype(np.float64)).astype(ml_dtypes.bfloat16)


def cas_table(length):
    index = np.arange(length)
    angle = (index[:, None] * index[None, :] % length) * (2.0 * np.pi / length)
    return np.cos(angle) + np.sin(angle)


def lane_table(table):
    high, low = high_low(table)
    out = np.zeros((2 * LANES, 2 * LANES), high.dtype)
    for row in (0, LANES):
        out[row : row + NZ, :NZ] = high
        out[row : row + NZ, LANES : LANES + NZ] = low
    return out


def row_table(table):
    high, low = high_low(table)
    return np.concatenate([np.concatenate([high, high], 1), np.concatenate([low, low], 1)], 0)


def plane_order(device):
    return np.concatenate([np.arange(SLAB_PLANES) + SLAB_PLANES * (device ^ k) for k in range(SLABS)])


def split(value):
    high = value.astype(bf16)
    return high, (value - high.astype(f32)).astype(bf16)


def product(left, right):
    return lax.dot_general(left, right, (((1,), (0,)), ((), ())), preferred_element_type=f32)


def along_lanes(value, table):
    both = product(jnp.concatenate(split(value), axis=1), table)
    return both[:, :LANES] + both[:, LANES:]


def along_rows(table, value):
    both = product(table, jnp.concatenate(split(value), axis=0))
    half = both.shape[0] // 2
    return both[:half] + both[half:]


def prepare_kernel(place, block, *refs):
    outs, natural = refs[:-1], refs[-1]
    me = place[0]

    def two_columns(step, carry):
        for a in range(GROUP):
            pair = [block[:, a, pl.ds(pl.multiple_of((2 * step + i) * LANES, LANES), LANES)] for i in range(2)]
            natural[a, pl.ds(pl.multiple_of(2 * SLAB_PLANES * step, 8), 2 * SLAB_PLANES), :] = jnp.concatenate(pair, 0)
        return carry

    lax.fori_loop(0, COLS // 2, two_columns, 0, unroll=2)
    for k in range(GROUP):
        outs[min(k, 2)][k // 3] = natural[(me & 3) ^ k]
        outs[3 + k][0] = natural[((me >> 2) * 2) ^ k]


def prepare(place, block):
    slabs = [jax.ShapeDtypeStruct((count, SLAB_ROWS, LANES), f32) for count in (1, 1, 2, 1, 1, 1, 1)]
    return pl.pallas_call(
        prepare_kernel,
        out_shape=slabs,
        in_specs=[in_smem, in_vmem],
        out_specs=[in_vmem] * 7,
        scratch_shapes=[pltpu.VMEM((GROUP, SLAB_ROWS, LANES), f32)],
        compiler_params=pltpu.CompilerParams(vmem_limit_bytes=32 << 20),
        cost_estimate=pl.CostEstimate(flops=0, bytes_accessed=6 << 20, transcendentals=0),
    )(place, block)


def tables_kernel(place, lanes_in, rows_in, forward_in, back_in, table_z, table_y, table_x, table_back, coulomb, sems):
    me = place[0]
    copies = [
        pltpu.make_async_copy(source, target, sems.at[i])
        for i, (source, target) in enumerate(
            ((lanes_in, table_z), (rows_in, table_y), (forward_in.at[me], table_x), (back_in.at[me], table_back))
        )
    ]
    for copy in copies:
        copy.start()
    scale = box_length * box_length / math.pi / (NX * NY * NZ)
    row = lax.broadcasted_iota(jnp.int32, (NY, LANES), 0)
    lane = lax.broadcasted_iota(jnp.int32, (NY, LANES), 1)
    plane = jnp.minimum(row, NY - row) ** 2 + jnp.minimum(lane, NZ - lane) ** 2
    plane = plane.astype(f32)

    def one_plane(x, carry):
        squares = plane + (x * x).astype(f32)
        coulomb[x] = jnp.where((squares > 0.5) & (lane < NZ), scale / jnp.maximum(squares, 1.0), 0.0)
        return carry

    lax.fori_loop(0, NX // 2 + 1, one_plane, 0)
    for copy in copies:
        copy.wait()


def make_tables(place, tables):
    return pl.pallas_call(
        tables_kernel,
        out_shape=[
            jax.ShapeDtypeStruct(tables[0].shape, bf16),
            *[jax.ShapeDtypeStruct(tables[1].shape, bf16)] * 3,
            jax.ShapeDtypeStruct((NX // 2 + 1, NY, LANES), f32),
        ],
        in_specs=[in_smem] + [pl.BlockSpec(memory_space=pl.ANY)] * 4,
        out_specs=[in_vmem] * 5,
        scratch_shapes=[pltpu.SemaphoreType.DMA((4,))],
        compiler_params=pltpu.CompilerParams(vmem_limit_bytes=16 << 20),
        cost_estimate=pl.CostEstimate(flops=0, bytes_accessed=1 << 20, transcendentals=0),
    )(place, *tables)


OWN_PLACES = ((0, 0), (4, 0), (1, 0), (4, 1), (2, 0), (4, 2), (3, 0), (5, 1))
VISITING_PLACES = (
    ((0, 0), (1, 0), (2, 0), (3, 0), (0, 1), (1, 1), (2, 1), (3, 1)),
    tuple((k, 0) for k in range(SLABS)),
)


def pair_kernel(turn, place, mask, *refs):
    places = VISITING_PLACES[turn]
    count = 1 + max(i for i, _ in places)
    own_refs, vis_refs, refs = refs[:6], refs[6 : 6 + count], refs[6 + count :]
    own_slabs = [own_refs[i].at[j] for i, j in OWN_PLACES]
    vis_slabs = [vis_refs[i].at[j] for i, j in places]
    table_z, table_y, table_x, table_back, coulomb, *refs = refs
    if turn:
        before, *refs = refs
        outs, refs = refs[:SLABS], refs[SLABS:]
    else:
        out, *refs = refs
    vis, spectrum = refs
    me = place[0]
    weight = -mask[me & 3, (me >> 2) * 2 + turn].astype(f32)

    def rows_of(step):
        return pl.ds(pl.multiple_of(2 * SLAB_PLANES * step, 8), 2 * SLAB_PLANES)

    def plane_of(y):
        return pl.ds(pl.multiple_of(y * PITCH, 8), NX)

    def columns_of(slabs, step):
        pieces = [slab[rows_of(step), :] for slab in slabs]
        return [
            jnp.concatenate([piece[:SLAB_PLANES] for piece in pieces], axis=0),
            jnp.concatenate([piece[SLAB_PLANES:] for piece in pieces], axis=0),
        ]

    def lane_index():
        return lax.broadcasted_iota(jnp.int32, (NX, LANES), 1)

    def forward(octet, carry):
        lane = lane_index()
        densities = []
        for i in range(3):
            step = 3 * octet + i
            pair = columns_of(vis_slabs, step)
            for j in range(2):
                vis[2 * step + j] = pair[j]
            densities += [a * b for a, b in zip(columns_of(own_slabs, step), pair)]
        for q in range(2):
            first, second, third = densities[3 * q : 3 * q + 3]
            rows = [
                first,
                pltpu.roll(jnp.where(lane >= 96, first, second), 32, 1),
                pltpu.roll(jnp.where(lane >= 64, second, third), 64, 1),
                pltpu.roll(third, 96, 1),
            ]
            done = along_lanes(jnp.concatenate(rows, axis=0), table_z[...])
            for j in range(2):
                both = [done[(2 * j + i) * NX : (2 * j + i + 1) * NX] for i in range(2)]
                both = along_rows(table_x[...], jnp.concatenate(both, axis=1))
                at = 8 * octet + 4 * q + 2 * j
                spectrum[plane_of(at), :] = both[:, :LANES]
                spectrum[plane_of(at + 1), :] = both[:, LANES:]
        return carry

    lax.fori_loop(0, OCTETS, forward, 0, unroll=UNROLL[0])

    def middle(step, carry):
        base = pl.multiple_of(8 * step, 8)
        for j in range(4):
            at = [base + 2 * j, base + 2 * j + 1]
            lines = [pl.ds(i, NY, stride=PITCH) for i in at]
            both = along_rows(table_y[...], jnp.concatenate([spectrum[line, :] for line in lines], axis=1))
            both = both * jnp.concatenate([coulomb[jnp.minimum(i, NX - i)] for i in at], axis=1)
            both = along_rows(table_y[...], both)
            for i, line in enumerate(lines):
                spectrum[line, :] = both[:, i * LANES : (i + 1) * LANES]
        return carry

    lax.fori_loop(0, NX // 8, middle, 0, unroll=UNROLL[1])

    def back(octet, carry):
        lane = lane_index()
        values = []
        for q in range(2):
            rows = []
            for j in range(2):
                at = 8 * octet + 4 * q + 2 * j
                both = along_rows(table_back[...], jnp.concatenate([spectrum[plane_of(at + i), :] for i in range(2)], axis=1))
                rows += [both[:, :LANES], both[:, LANES:]]
            done = along_lanes(jnp.concatenate(rows, axis=0), table_z[...])
            first, second, third, fourth = [done[NX * i : NX * (i + 1)] for i in range(4)]
            second = pltpu.roll(second, 96, 1)
            third = pltpu.roll(third, 64, 1)
            fourth = pltpu.roll(fourth, 32, 1)
            columns = (
                jnp.where(lane < 96, first, second),
                jnp.where(lane < 64, second, third),
                jnp.where(lane < 32, third, fourth),
            )
            for i in range(3):
                at = 6 * octet + 3 * q + i
                value = weight * (columns[i] * vis[at])
                if turn:
                    values.append(before[at] + value)
                else:
                    out[at] = value
        if turn:
            for i in range(3):
                even, odd = values[2 * i : 2 * i + 2]
                for k in range(SLABS):
                    cut = slice(SLAB_PLANES * k, SLAB_PLANES * (k + 1))
                    outs[k][rows_of(3 * octet + i), :] = jnp.concatenate([even[cut], odd[cut]], axis=0)
        return carry

    lax.fori_loop(0, OCTETS, back, 0, unroll=UNROLL[2])


def pair_step(turn, place, mask, own, visiting, tables, before=None):
    extra = [] if before is None else [before]
    whole = jax.ShapeDtypeStruct((COLS, NX, LANES), f32)
    slab = jax.ShapeDtypeStruct((SLAB_ROWS, LANES), f32)
    return pl.pallas_call(
        functools.partial(pair_kernel, turn),
        out_shape=[slab] * SLABS if turn else whole,
        in_specs=[in_smem] * 2 + [in_vmem] * (len(own) + len(visiting) + 5 + len(extra)),
        out_specs=[in_vmem] * SLABS if turn else in_vmem,
        scratch_shapes=[
            pltpu.VMEM((COLS, NX, LANES), f32),
            pltpu.VMEM((NY * PITCH, LANES), f32),
        ],
        compiler_params=pltpu.CompilerParams(vmem_limit_bytes=PAIR_VMEM),
        cost_estimate=pl.CostEstimate(flops=0, bytes_accessed=1 << 20, transcendentals=0),
    )(place, mask, *own, *visiting, *tables, *extra)


def gram_kernel(place, *refs):
    parts, refs = refs[:SLABS], refs[SLABS:]
    own, refs = refs[:3], refs[3:]
    natural, gram = refs
    me = place[0] & 3
    for k in range(GROUP):
        natural[me ^ k] = parts[k][...] + parts[k + GROUP][...]
    for a in range(GROUP):
        for c in range(GROUP):
            terms = own[min(a, 2)][a // 3] * natural[me ^ c]
            terms = jnp.sum(terms.reshape(SLAB_ROWS // 8, 8, LANES), axis=0)
            gram[(me ^ a) * GROUP + (me ^ c)] = jnp.sum(terms, axis=0, keepdims=True)


def layout_kernel(natural, out):
    def two_columns(step, carry):
        rows = pl.ds(pl.multiple_of(2 * SLAB_PLANES * step, 8), 2 * SLAB_PLANES)
        for a in range(GROUP):
            pair = natural[a, rows, :]
            for i in range(2):
                lanes = pl.ds(pl.multiple_of((2 * step + i) * LANES, LANES), LANES)
                out[:, a, lanes] = pair[SLAB_PLANES * i : SLAB_PLANES * (i + 1)]
        return carry

    lax.fori_loop(0, COLS // 2, two_columns, 0, unroll=2)


def finish(place, parts, own):
    natural, gram = pl.pallas_call(
        gram_kernel,
        out_shape=[
            jax.ShapeDtypeStruct((GROUP, SLAB_ROWS, LANES), f32),
            jax.ShapeDtypeStruct((GROUP * GROUP, 1, LANES), f32),
        ],
        in_specs=[in_smem] + [in_vmem] * (SLABS + 3),
        out_specs=[in_vmem] * 2,
        compiler_params=pltpu.CompilerParams(vmem_limit_bytes=32 << 20),
        cost_estimate=pl.CostEstimate(flops=0, bytes_accessed=8 << 20, transcendentals=0),
    )(place, *parts, *own)
    field = pl.pallas_call(
        layout_kernel,
        out_shape=jax.ShapeDtypeStruct((SLAB_PLANES, GROUP, NY * NZ), f32),
        in_specs=[in_vmem],
        out_specs=in_vmem,
        compiler_params=pltpu.CompilerParams(vmem_limit_bytes=32 << 20),
        cost_estimate=pl.CostEstimate(flops=0, bytes_accessed=8 << 20, transcendentals=0),
    )(natural)
    gram = jnp.sum(gram.reshape(GROUP, GROUP, LANES), axis=2) / (NX * NY * NZ)
    gram = gram + to_partner(gram, 1)
    gram = (gram + to_partner(gram, 2)) + (to_partner(gram, 4) + to_partner(gram, 6))
    return field, gram


def to_partner(block, flip):
    return lax.ppermute(block, "grid", [(i, i ^ flip) for i in range(SLABS)])


def to_group(block, distance, flip):
    bands = lax.axis_size("band")
    route = [(b * SLABS + i, (b + distance) % bands * SLABS + (i ^ flip)) for b in range(bands) for i in range(SLABS)]
    return lax.ppermute(block, ("band", "grid"), route)


def after(value, *others):
    return lax.optimization_barrier((value, *others))[0]


def pair_plan(orbitals, pair_mask, cycle_step):
    me = lax.axis_index("grid")
    place = me.astype(jnp.int32).reshape(1)
    cas = cas_table(NX)
    forward_x = jnp.asarray(np.stack([row_table(cas[:, plane_order(d)]) for d in range(SLABS)]))
    back_x = jnp.asarray(np.stack([row_table(cas[plane_order(d), :]) for d in range(SLABS)]))
    fixed = jnp.asarray(lane_table(cas)), jnp.asarray(row_table(cas)), forward_x, back_x
    slabs = prepare(place, jnp.transpose(orbitals, (1, 0, 2)))

    bands = lax.axis_size("band")

    def with_distance(distance, slabs, pair_mask, place, fixed):
        own_out, vis_out = slabs[:3], slabs[3:]
        own_y = to_partner(own_out[0], 4)
        across = to_group(vis_out[2], distance, 4)
        home = to_group(vis_out[0], distance, 0)
        own_next = to_partner(own_out[1], 4)
        own_x = to_partner(own_out[2], 2)
        near = min(distance, bands - distance) == 1
        first = jnp.concatenate([after(home, own_x, own_y), across])
        first_x = to_partner(first, 2)
        across = to_group(after(vis_out[3], first), distance, 4)
        home = to_group(after(vis_out[1], first if near else across), distance, 0)
        tables = make_tables(after(place, first), fixed)
        if near:
            own_far = to_partner(after(own_x, across, own_next, *tables), 4)
            home_x, across_x = to_partner(home, 2), to_partner(across, 2)
            ready, last = home, home_x
        else:
            own_far = to_partner(after(own_x, own_next, *tables), 4)
            ready = last = across
        crossing = jnp.concatenate([after(own_out[1], ready if not near else first), own_x[1:], own_next])
        crossed, far_crossed = to_partner(crossing, 1), to_partner(after(own_far, last), 1)
        first_core, beside_core = to_partner(after(first, ready), 1), to_partner(after(first_x, ready), 1)
        own = [own_out[0], own_x, own_y, own_far, crossed, far_crossed]
        visiting = [first, first_core, first_x, beside_core]
        total = pair_step(0, place, pair_mask, own, visiting, tables)
        if not near:
            home_x, across_x = to_partner(after(home, total), 2), to_partner(across, 2)
        cores = [to_partner(slab, 1) for slab in (home, home_x, across)]
        cores.append(to_partner(after(across_x, total), 1))
        visiting = [home, cores[0], home_x, cores[1], across, cores[2], across_x, cores[3]]
        parts = pair_step(1, place, pair_mask, own, visiting, tables, total)
        parts = [parts[0]] + [to_partner(parts[k], k) for k in range(1, SLABS)]
        return finish(place, parts, own_out)

    field, gram = lax.switch(
        cycle_step - 1,
        [functools.partial(with_distance, distance) for distance in range(1, bands)],
        slabs,
        pair_mask,
        place,
        fixed,
    )
    return jnp.transpose(field, (1, 0, 2)), gram


def shards(orbitals, pair_mask, cycle_step):
    if lax.axis_size("grid") == SLABS and orbitals.shape[0] == GROUP:
        return pair_plan(orbitals, pair_mask, cycle_step)
    return slab_plan(orbitals, pair_mask, cycle_step)


def solution(mesh):
    return jax.shard_map(
        shards,
        mesh=mesh,
        in_specs=(P("band", "grid", None), P("band", None), P()),
        out_specs=(P("band", "grid", None), P("band", None)),
        check_vma=False,
    )
```

```python
import functools
import math

import jax
import jax.numpy as jnp
import ml_dtypes
import numpy as np
from jax import lax
from jax.experimental import pallas as pl
from jax.experimental.pallas import tpu as pltpu
from jax.sharding import PartitionSpec as P

NX = 96
NY = 96
NZ = 96
LANES = 128


box_length = 16.0
highest = lax.Precision.HIGHEST


def passed_along(block, axis, distance):
    devices = range(lax.axis_size(axis))
    route = [((i - distance) % len(devices), i) for i in devices]
    return lax.ppermute(block, axis, route)


def hartley_table(length):
    index = jnp.arange(length, dtype=jnp.int32)
    product = index[:, None] * index[None, :] % length
    angle = product.astype(jnp.float32) * (2.0 * math.pi / length)
    return jnp.cos(angle) + jnp.sin(angle)


def folded(index, length):
    return jnp.where(index * 2 >= length, index - length, index).astype(jnp.float32)


def across_planes(field, table_y, table_z):
    count = field.shape[0]
    planes = field.shape[1]
    shaped = field.reshape(count * planes * NY, NZ)
    shaped = jnp.matmul(shaped, table_z, precision=highest)
    shaped = shaped.reshape(count * planes, NY, NZ)
    shaped = jnp.matmul(table_y, shaped, precision=highest)
    return shaped.reshape(count, planes, NY * NZ)


def slab_plan(orbitals, pair_mask, cycle_step):
    orbit_count = orbitals.shape[0]
    planes = orbitals.shape[1]
    grid_count = lax.axis_size("grid")
    slab_rows = NY // grid_count

    def one_hop(turn, block):
        return passed_along(block, "band", 1)

    visiting = lax.fori_loop(0, cycle_step, one_hop, orbitals)
    table_x = hartley_table(NX)
    table_y = hartley_table(NY)
    table_z = hartley_table(NZ)
    row_index = lax.axis_index("grid") * slab_rows + jnp.arange(slab_rows, dtype=jnp.int32)
    freq_x = folded(jnp.arange(NX, dtype=jnp.int32), NX)
    freq_y = folded(row_index, NY)
    freq_z = folded(jnp.arange(NZ, dtype=jnp.int32), NZ)
    squares = freq_x[:, None, None] ** 2 + freq_y[None, :, None] ** 2 + freq_z[None, None, :] ** 2
    coulomb = box_length * box_length / math.pi / (NX * NY * NZ)
    kernel = jnp.where(squares > 0.5, coulomb / jnp.maximum(squares, 1.0), jnp.float32(0.0))
    kernel = kernel.reshape(NX, slab_rows * NZ)

    def solve_items(spectra):
        along = jnp.matmul(table_x, spectra, precision=highest) * kernel
        along = jnp.matmul(table_x, along, precision=highest)
        return lax.all_to_all(along, "grid", split_axis=1, concat_axis=2, tiled=True)

    mask_float = pair_mask.astype(jnp.float32).reshape(
        orbit_count // orbit_count, orbit_count, orbit_count
    )
    own_rows = orbitals.reshape(orbit_count // orbit_count, orbit_count, planes, NY * NZ)

    def one_group(carry, inputs):
        rows, weights = inputs
        density = (rows[:, None] * visiting[None]).reshape(
            orbit_count * orbit_count, planes, NY * NZ
        )
        spectra = across_planes(density, table_y, table_z)
        potential = solve_items(
            lax.all_to_all(spectra, "grid", split_axis=2, concat_axis=1, tiled=True)
        )
        potential = across_planes(potential, table_y, table_z)
        potential = potential.reshape(orbit_count, orbit_count, planes, NY * NZ)
        field = -jnp.einsum("aj,ajxr->axr", weights, potential * visiting[None], precision=highest)
        return (carry, field)

    start_carry = jnp.zeros((), jnp.float32)
    _, fields = lax.scan(one_group, start_carry, (own_rows, mask_float))
    exchange_field = fields.reshape(orbit_count, planes, NY * NZ)
    local_terms = jnp.einsum("axr,cxr->ac", orbitals, exchange_field, precision=highest) / (
        NX * NY * NZ
    )
    projection = lax.psum(local_terms, "grid")
    return (exchange_field, projection)


SLABS = 8
GROUP = 4
SLAB_PLANES = NX // SLABS
COLS = NY * NZ // LANES
SLAB_ROWS = SLAB_PLANES * COLS
OCTETS = NY // 8
PITCH = NX + 8
UNROLL = (6, 4, 4)
PAIR_VMEM = 36 << 20

bf16 = jnp.bfloat16
f32 = jnp.float32
in_vmem = pl.BlockSpec(memory_space=pltpu.VMEM)
in_smem = pl.BlockSpec(memory_space=pltpu.SMEM)


def high_low(table):
    high = table.astype(ml_dtypes.bfloat16)
    return high, (table - high.astype(np.float64)).astype(ml_dtypes.bfloat16)


def cas_table(length):
    index = np.arange(length)
    angle = (index[:, None] * index[None, :] % length) * (2.0 * np.pi / length)
    return np.cos(angle) + np.sin(angle)


def lane_table(table):
    high, low = high_low(table)
    out = np.zeros((2 * LANES, 2 * LANES), high.dtype)
    for row in (0, LANES):
        out[row : row + NZ, :NZ] = high
        out[row : row + NZ, LANES : LANES + NZ] = low
    return out


def row_table(table):
    high, low = high_low(table)
    return np.concatenate([np.concatenate([high, high], 1), np.concatenate([low, low], 1)], 0)


def plane_order(device):
    return np.concatenate([np.arange(SLAB_PLANES) + SLAB_PLANES * (device ^ k) for k in range(SLABS)])


def split(value):
    high = value.astype(bf16)
    return high, (value - high.astype(f32)).astype(bf16)


def product(left, right):
    return lax.dot_general(left, right, (((1,), (0,)), ((), ())), preferred_element_type=f32)


def along_lanes(value, table):
    both = product(jnp.concatenate(split(value), axis=1), table)
    return both[:, :LANES] + both[:, LANES:]


def along_rows(table, value):
    both = product(table, jnp.concatenate(split(value), axis=0))
    half = both.shape[0] // 2
    return both[:half] + both[half:]


def prepare_kernel(place, block, *refs):
    outs, natural = refs[:-1], refs[-1]
    me = place[0]

    def two_columns(step, carry):
        for a in range(GROUP):
            pair = [block[:, a, pl.ds(pl.multiple_of((2 * step + i) * LANES, LANES), LANES)] for i in range(2)]
            natural[a, pl.ds(pl.multiple_of(2 * SLAB_PLANES * step, 8), 2 * SLAB_PLANES), :] = jnp.concatenate(pair, 0)
        return carry

    lax.fori_loop(0, COLS // 2, two_columns, 0, unroll=2)
    for k in range(GROUP):
        outs[min(k, 2)][k // 3] = natural[(me & 3) ^ k]
        outs[3 + k][0] = natural[((me >> 2) * 2) ^ k]


def prepare(place, block):
    slabs = [jax.ShapeDtypeStruct((count, SLAB_ROWS, LANES), f32) for count in (1, 1, 2, 1, 1, 1, 1)]
    return pl.pallas_call(
        prepare_kernel,
        out_shape=slabs,
        in_specs=[in_smem, in_vmem],
        out_specs=[in_vmem] * 7,
        scratch_shapes=[pltpu.VMEM((GROUP, SLAB_ROWS, LANES), f32)],
        compiler_params=pltpu.CompilerParams(vmem_limit_bytes=32 << 20),
        cost_estimate=pl.CostEstimate(flops=0, bytes_accessed=6 << 20, transcendentals=0),
    )(place, block)


def tables_kernel(place, lanes_in, rows_in, forward_in, back_in, table_z, table_y, table_x, table_back, coulomb, sems):
    me = place[0]
    copies = [
        pltpu.make_async_copy(source, target, sems.at[i])
        for i, (source, target) in enumerate(
            ((lanes_in, table_z), (rows_in, table_y), (forward_in.at[me], table_x), (back_in.at[me], table_back))
        )
    ]
    for copy in copies:
        copy.start()
    scale = box_length * box_length / math.pi / (NX * NY * NZ)
    row = lax.broadcasted_iota(jnp.int32, (NY, LANES), 0)
    lane = lax.broadcasted_iota(jnp.int32, (NY, LANES), 1)
    plane = jnp.minimum(row, NY - row) ** 2 + jnp.minimum(lane, NZ - lane) ** 2
    plane = plane.astype(f32)

    def one_plane(x, carry):
        squares = plane + (x * x).astype(f32)
        coulomb[x] = jnp.where((squares > 0.5) & (lane < NZ), scale / jnp.maximum(squares, 1.0), 0.0)
        return carry

    lax.fori_loop(0, NX // 2 + 1, one_plane, 0)
    for copy in copies:
        copy.wait()


def make_tables(place, tables):
    return pl.pallas_call(
        tables_kernel,
        out_shape=[
            jax.ShapeDtypeStruct(tables[0].shape, bf16),
            *[jax.ShapeDtypeStruct(tables[1].shape, bf16)] * 3,
            jax.ShapeDtypeStruct((NX // 2 + 1, NY, LANES), f32),
        ],
        in_specs=[in_smem] + [pl.BlockSpec(memory_space=pl.ANY)] * 4,
        out_specs=[in_vmem] * 5,
        scratch_shapes=[pltpu.SemaphoreType.DMA((4,))],
        compiler_params=pltpu.CompilerParams(vmem_limit_bytes=16 << 20),
        cost_estimate=pl.CostEstimate(flops=0, bytes_accessed=1 << 20, transcendentals=0),
    )(place, *tables)


OWN_PLACES = ((0, 0), (4, 0), (1, 0), (4, 1), (2, 0), (4, 2), (3, 0), (5, 1))
VISITING_PLACES = (
    ((0, 0), (1, 0), (2, 0), (3, 0), (0, 1), (1, 1), (2, 1), (3, 1)),
    tuple((k, 0) for k in range(SLABS)),
)


def pair_kernel(turn, place, mask, *refs):
    places = VISITING_PLACES[turn]
    count = 1 + max(i for i, _ in places)
    own_refs, vis_refs, refs = refs[:6], refs[6 : 6 + count], refs[6 + count :]
    own_slabs = [own_refs[i].at[j] for i, j in OWN_PLACES]
    vis_slabs = [vis_refs[i].at[j] for i, j in places]
    table_z, table_y, table_x, table_back, coulomb, *refs = refs
    if turn:
        before, *refs = refs
        outs, refs = refs[:SLABS], refs[SLABS:]
    else:
        out, *refs = refs
    vis, spectrum = refs
    me = place[0]
    weight = -mask[me & 3, (me >> 2) * 2 + turn].astype(f32)

    def rows_of(step):
        return pl.ds(pl.multiple_of(2 * SLAB_PLANES * step, 8), 2 * SLAB_PLANES)

    def plane_of(y):
        return pl.ds(pl.multiple_of(y * PITCH, 8), NX)

    def columns_of(slabs, step):
        pieces = [slab[rows_of(step), :] for slab in slabs]
        return [
            jnp.concatenate([piece[:SLAB_PLANES] for piece in pieces], axis=0),
            jnp.concatenate([piece[SLAB_PLANES:] for piece in pieces], axis=0),
        ]

    def lane_index():
        return lax.broadcasted_iota(jnp.int32, (NX, LANES), 1)

    def forward(octet, carry):
        lane = lane_index()
        densities = []
        for i in range(3):
            step = 3 * octet + i
            pair = columns_of(vis_slabs, step)
            for j in range(2):
                vis[2 * step + j] = pair[j]
            densities += [a * b for a, b in zip(columns_of(own_slabs, step), pair)]
        for q in range(2):
            first, second, third = densities[3 * q : 3 * q + 3]
            rows = [
                first,
                pltpu.roll(jnp.where(lane >= 96, first, second), 32, 1),
                pltpu.roll(jnp.where(lane >= 64, second, third), 64, 1),
                pltpu.roll(third, 96, 1),
            ]
            done = along_lanes(jnp.concatenate(rows, axis=0), table_z[...])
            for j in range(2):
                both = [done[(2 * j + i) * NX : (2 * j + i + 1) * NX] for i in range(2)]
                both = along_rows(table_x[...], jnp.concatenate(both, axis=1))
                at = 8 * octet + 4 * q + 2 * j
                spectrum[plane_of(at), :] = both[:, :LANES]
                spectrum[plane_of(at + 1), :] = both[:, LANES:]
        return carry

    lax.fori_loop(0, OCTETS, forward, 0, unroll=UNROLL[0])

    def middle(step, carry):
        base = pl.multiple_of(8 * step, 8)
        for j in range(4):
            at = [base + 2 * j, base + 2 * j + 1]
            lines = [pl.ds(i, NY, stride=PITCH) for i in at]
            both = along_rows(table_y[...], jnp.concatenate([spectrum[line, :] for line in lines], axis=1))
            both = both * jnp.concatenate([coulomb[jnp.minimum(i, NX - i)] for i in at], axis=1)
            both = along_rows(table_y[...], both)
            for i, line in enumerate(lines):
                spectrum[line, :] = both[:, i * LANES : (i + 1) * LANES]
        return carry

    lax.fori_loop(0, NX // 8, middle, 0, unroll=UNROLL[1])

    def back(octet, carry):
        lane = lane_index()
        values = []
        for q in range(2):
            rows = []
            for j in range(2):
                at = 8 * octet + 4 * q + 2 * j
                both = along_rows(table_back[...], jnp.concatenate([spectrum[plane_of(at + i), :] for i in range(2)], axis=1))
                rows += [both[:, :LANES], both[:, LANES:]]
            done = along_lanes(jnp.concatenate(rows, axis=0), table_z[...])
            first, second, third, fourth = [done[NX * i : NX * (i + 1)] for i in range(4)]
            second = pltpu.roll(second, 96, 1)
            third = pltpu.roll(third, 64, 1)
            fourth = pltpu.roll(fourth, 32, 1)
            columns = (
                jnp.where(lane < 96, first, second),
                jnp.where(lane < 64, second, third),
                jnp.where(lane < 32, third, fourth),
            )
            for i in range(3):
                at = 6 * octet + 3 * q + i
                value = weight * (columns[i] * vis[at])
                if turn:
                    values.append(before[at] + value)
                else:
                    out[at] = value
        if turn:
            for i in range(3):
                even, odd = values[2 * i : 2 * i + 2]
                for k in range(SLABS):
                    cut = slice(SLAB_PLANES * k, SLAB_PLANES * (k + 1))
                    outs[k][rows_of(3 * octet + i), :] = jnp.concatenate([even[cut], odd[cut]], axis=0)
        return carry

    lax.fori_loop(0, OCTETS, back, 0, unroll=UNROLL[2])


def pair_step(turn, place, mask, own, visiting, tables, before=None):
    extra = [] if before is None else [before]
    whole = jax.ShapeDtypeStruct((COLS, NX, LANES), f32)
    slab = jax.ShapeDtypeStruct((SLAB_ROWS, LANES), f32)
    return pl.pallas_call(
        functools.partial(pair_kernel, turn),
        out_shape=[slab] * SLABS if turn else whole,
        in_specs=[in_smem] * 2 + [in_vmem] * (len(own) + len(visiting) + 5 + len(extra)),
        out_specs=[in_vmem] * SLABS if turn else in_vmem,
        scratch_shapes=[
            pltpu.VMEM((COLS, NX, LANES), f32),
            pltpu.VMEM((NY * PITCH, LANES), f32),
        ],
        compiler_params=pltpu.CompilerParams(vmem_limit_bytes=PAIR_VMEM),
        cost_estimate=pl.CostEstimate(flops=0, bytes_accessed=1 << 20, transcendentals=0),
    )(place, mask, *own, *visiting, *tables, *extra)


def gram_kernel(place, *refs):
    parts, refs = refs[:SLABS], refs[SLABS:]
    own, refs = refs[:3], refs[3:]
    natural, gram = refs
    me = place[0] & 3
    for k in range(GROUP):
        natural[me ^ k] = parts[k][...] + parts[k + GROUP][...]
    for a in range(GROUP):
        for c in range(GROUP):
            terms = own[min(a, 2)][a // 3] * natural[me ^ c]
            terms = jnp.sum(terms.reshape(SLAB_ROWS // 8, 8, LANES), axis=0)
            gram[(me ^ a) * GROUP + (me ^ c)] = jnp.sum(terms, axis=0, keepdims=True)


def layout_kernel(natural, out):
    def two_columns(step, carry):
        rows = pl.ds(pl.multiple_of(2 * SLAB_PLANES * step, 8), 2 * SLAB_PLANES)
        for a in range(GROUP):
            pair = natural[a, rows, :]
            for i in range(2):
                lanes = pl.ds(pl.multiple_of((2 * step + i) * LANES, LANES), LANES)
                out[:, a, lanes] = pair[SLAB_PLANES * i : SLAB_PLANES * (i + 1)]
        return carry

    lax.fori_loop(0, COLS // 2, two_columns, 0, unroll=2)


def finish(place, parts, own):
    natural, gram = pl.pallas_call(
        gram_kernel,
        out_shape=[
            jax.ShapeDtypeStruct((GROUP, SLAB_ROWS, LANES), f32),
            jax.ShapeDtypeStruct((GROUP * GROUP, 1, LANES), f32),
        ],
        in_specs=[in_smem] + [in_vmem] * (SLABS + 3),
        out_specs=[in_vmem] * 2,
        compiler_params=pltpu.CompilerParams(vmem_limit_bytes=32 << 20),
        cost_estimate=pl.CostEstimate(flops=0, bytes_accessed=8 << 20, transcendentals=0),
    )(place, *parts, *own)
    field = pl.pallas_call(
        layout_kernel,
        out_shape=jax.ShapeDtypeStruct((SLAB_PLANES, GROUP, NY * NZ), f32),
        in_specs=[in_vmem],
        out_specs=in_vmem,
        compiler_params=pltpu.CompilerParams(vmem_limit_bytes=32 << 20),
        cost_estimate=pl.CostEstimate(flops=0, bytes_accessed=8 << 20, transcendentals=0),
    )(natural)
    gram = jnp.sum(gram.reshape(GROUP, GROUP, LANES), axis=2) / (NX * NY * NZ)
    gram = gram + to_partner(gram, 1)
    gram = (gram + to_partner(gram, 2)) + (to_partner(gram, 4) + to_partner(gram, 6))
    return field, gram


def to_partner(block, flip):
    return lax.ppermute(block, "grid", [(i, i ^ flip) for i in range(SLABS)])


def to_group(block, distance, flip):
    bands = lax.axis_size("band")
    route = [(b * SLABS + i, (b + distance) % bands * SLABS + (i ^ flip)) for b in range(bands) for i in range(SLABS)]
    return lax.ppermute(block, ("band", "grid"), route)


def after(value, *others):
    return lax.optimization_barrier((value, *others))[0]


def pair_plan(orbitals, pair_mask, cycle_step):
    me = lax.axis_index("grid")
    place = me.astype(jnp.int32).reshape(1)
    cas = cas_table(NX)
    forward_x = jnp.asarray(np.stack([row_table(cas[:, plane_order(d)]) for d in range(SLABS)]))
    back_x = jnp.asarray(np.stack([row_table(cas[plane_order(d), :]) for d in range(SLABS)]))
    fixed = jnp.asarray(lane_table(cas)), jnp.asarray(row_table(cas)), forward_x, back_x
    slabs = prepare(place, jnp.transpose(orbitals, (1, 0, 2)))

    bands = lax.axis_size("band")

    def with_distance(distance, slabs, pair_mask, place, fixed):
        own_out, vis_out = slabs[:3], slabs[3:]
        own_y = to_partner(own_out[0], 4)
        across = to_group(vis_out[2], distance, 4)
        home = to_group(vis_out[0], distance, 0)
        own_next = to_partner(own_out[1], 4)
        own_x = to_partner(own_out[2], 2)
        near = min(distance, bands - distance) == 1
        first = jnp.concatenate([after(home, own_x, own_y), across])
        first_x = to_partner(first, 2)
        across = to_group(after(vis_out[3], first), distance, 4)
        home = to_group(after(vis_out[1], first if near else across), distance, 0)
        tables = make_tables(after(place, first), fixed)
        if near:
            own_far = to_partner(after(own_x, across, own_next, *tables), 4)
            home_x, across_x = to_partner(home, 2), to_partner(across, 2)
            ready, last = home, home_x
        else:
            own_far = to_partner(after(own_x, own_next, *tables), 4)
            ready = last = across
        crossing = jnp.concatenate([after(own_out[1], ready if not near else first), own_x[1:], own_next])
        crossed, far_crossed = to_partner(crossing, 1), to_partner(after(own_far, last), 1)
        first_core, beside_core = to_partner(after(first, ready), 1), to_partner(after(first_x, ready), 1)
        own = [own_out[0], own_x, own_y, own_far, crossed, far_crossed]
        visiting = [first, first_core, first_x, beside_core]
        total = pair_step(0, place, pair_mask, own, visiting, tables)
        if not near:
            home_x, across_x = to_partner(after(home, total), 2), to_partner(across, 2)
        cores = [to_partner(slab, 1) for slab in (home, home_x, across)]
        cores.append(to_partner(after(across_x, total), 1))
        visiting = [home, cores[0], home_x, cores[1], across, cores[2], across_x, cores[3]]
        parts = pair_step(1, place, pair_mask, own, visiting, tables, total)
        parts = [parts[0]] + [to_partner(parts[k], k) for k in range(1, SLABS)]
        return finish(place, parts, own_out)

    field, gram = lax.switch(
        cycle_step - 1,
        [functools.partial(with_distance, distance) for distance in range(1, bands)],
        slabs,
        pair_mask,
        place,
        fixed,
    )
    return jnp.transpose(field, (1, 0, 2)), gram


def shards(orbitals, pair_mask, cycle_step):
    if lax.axis_size("grid") == SLABS and orbitals.shape[0] == GROUP:
        return pair_plan(orbitals, pair_mask, cycle_step)
    return slab_plan(orbitals, pair_mask, cycle_step)


def solution(mesh):
    return jax.shard_map(
        shards,
        mesh=mesh,
        in_specs=(P("band", "grid", None), P("band", None), P()),
        out_specs=(P("band", "grid", None), P("band", None)),
        check_vma=False,
    )
```

```python
import functools
import math

import jax
import jax.numpy as jnp
import ml_dtypes
import numpy as np
from jax import lax
from jax.experimental import pallas as pl
from jax.experimental.pallas import tpu as pltpu
from jax.sharding import PartitionSpec as P

NX = 96
NY = 96
NZ = 96
LANES = 128


box_length = 16.0
highest = lax.Precision.HIGHEST


def passed_along(block, axis, distance):
    devices = range(lax.axis_size(axis))
    route = [((i - distance) % len(devices), i) for i in devices]
    return lax.ppermute(block, axis, route)


def hartley_table(length):
    index = jnp.arange(length, dtype=jnp.int32)
    product = index[:, None] * index[None, :] % length
    angle = product.astype(jnp.float32) * (2.0 * math.pi / length)
    return jnp.cos(angle) + jnp.sin(angle)


def folded(index, length):
    return jnp.where(index * 2 >= length, index - length, index).astype(jnp.float32)


def across_planes(field, table_y, table_z):
    count = field.shape[0]
    planes = field.shape[1]
    shaped = field.reshape(count * planes * NY, NZ)
    shaped = jnp.matmul(shaped, table_z, precision=highest)
    shaped = shaped.reshape(count * planes, NY, NZ)
    shaped = jnp.matmul(table_y, shaped, precision=highest)
    return shaped.reshape(count, planes, NY * NZ)


def slab_plan(orbitals, pair_mask, cycle_step):
    orbit_count = orbitals.shape[0]
    planes = orbitals.shape[1]
    grid_count = lax.axis_size("grid")
    slab_rows = NY // grid_count

    def one_hop(turn, block):
        return passed_along(block, "band", 1)

    visiting = lax.fori_loop(0, cycle_step, one_hop, orbitals)
    table_x = hartley_table(NX)
    table_y = hartley_table(NY)
    table_z = hartley_table(NZ)
    row_index = lax.axis_index("grid") * slab_rows + jnp.arange(slab_rows, dtype=jnp.int32)
    freq_x = folded(jnp.arange(NX, dtype=jnp.int32), NX)
    freq_y = folded(row_index, NY)
    freq_z = folded(jnp.arange(NZ, dtype=jnp.int32), NZ)
    squares = freq_x[:, None, None] ** 2 + freq_y[None, :, None] ** 2 + freq_z[None, None, :] ** 2
    coulomb = box_length * box_length / math.pi / (NX * NY * NZ)
    kernel = jnp.where(squares > 0.5, coulomb / jnp.maximum(squares, 1.0), jnp.float32(0.0))
    kernel = kernel.reshape(NX, slab_rows * NZ)

    def solve_items(spectra):
        along = jnp.matmul(table_x, spectra, precision=highest) * kernel
        along = jnp.matmul(table_x, along, precision=highest)
        return lax.all_to_all(along, "grid", split_axis=1, concat_axis=2, tiled=True)

    mask_float = pair_mask.astype(jnp.float32).reshape(
        orbit_count // orbit_count, orbit_count, orbit_count
    )
    own_rows = orbitals.reshape(orbit_count // orbit_count, orbit_count, planes, NY * NZ)

    def one_group(carry, inputs):
        rows, weights = inputs
        density = (rows[:, None] * visiting[None]).reshape(
            orbit_count * orbit_count, planes, NY * NZ
        )
        spectra = across_planes(density, table_y, table_z)
        potential = solve_items(
            lax.all_to_all(spectra, "grid", split_axis=2, concat_axis=1, tiled=True)
        )
        potential = across_planes(potential, table_y, table_z)
        potential = potential.reshape(orbit_count, orbit_count, planes, NY * NZ)
        field = -jnp.einsum("aj,ajxr->axr", weights, potential * visiting[None], precision=highest)
        return (carry, field)

    start_carry = jnp.zeros((), jnp.float32)
    _, fields = lax.scan(one_group, start_carry, (own_rows, mask_float))
    exchange_field = fields.reshape(orbit_count, planes, NY * NZ)
    local_terms = jnp.einsum("axr,cxr->ac", orbitals, exchange_field, precision=highest) / (
        NX * NY * NZ
    )
    projection = lax.psum(local_terms, "grid")
    return (exchange_field, projection)


SLABS = 8
GROUP = 4
SLAB_PLANES = NX // SLABS
COLS = NY * NZ // LANES
SLAB_ROWS = SLAB_PLANES * COLS
OCTETS = NY // 8
PITCH = NX + 8
UNROLL = (6, 4, 4)
PAIR_VMEM = 36 << 20

bf16 = jnp.bfloat16
f32 = jnp.float32
in_vmem = pl.BlockSpec(memory_space=pltpu.VMEM)
in_smem = pl.BlockSpec(memory_space=pltpu.SMEM)


def high_low(table):
    high = table.astype(ml_dtypes.bfloat16)
    return high, (table - high.astype(np.float64)).astype(ml_dtypes.bfloat16)


def cas_table(length):
    index = np.arange(length)
    angle = (index[:, None] * index[None, :] % length) * (2.0 * np.pi / length)
    return np.cos(angle) + np.sin(angle)


def lane_table(table):
    high, low = high_low(table)
    out = np.zeros((2 * LANES, 2 * LANES), high.dtype)
    for row in (0, LANES):
        out[row : row + NZ, :NZ] = high
        out[row : row + NZ, LANES : LANES + NZ] = low
    return out


def row_table(table):
    high, low = high_low(table)
    return np.concatenate([np.concatenate([high, high], 1), np.concatenate([low, low], 1)], 0)


def plane_order(device):
    return np.concatenate([np.arange(SLAB_PLANES) + SLAB_PLANES * (device ^ k) for k in range(SLABS)])


def split(value):
    high = value.astype(bf16)
    return high, (value - high.astype(f32)).astype(bf16)


def product(left, right):
    return lax.dot_general(left, right, (((1,), (0,)), ((), ())), preferred_element_type=f32)


def along_lanes(value, table):
    both = product(jnp.concatenate(split(value), axis=1), table)
    return both[:, :LANES] + both[:, LANES:]


def along_rows(table, value):
    both = product(table, jnp.concatenate(split(value), axis=0))
    half = both.shape[0] // 2
    return both[:half] + both[half:]


def prepare_kernel(place, block, *refs):
    outs, natural = refs[:-1], refs[-1]
    me = place[0]

    def two_columns(step, carry):
        for a in range(GROUP):
            pair = [block[:, a, pl.ds(pl.multiple_of((2 * step + i) * LANES, LANES), LANES)] for i in range(2)]
            natural[a, pl.ds(pl.multiple_of(2 * SLAB_PLANES * step, 8), 2 * SLAB_PLANES), :] = jnp.concatenate(pair, 0)
        return carry

    lax.fori_loop(0, COLS // 2, two_columns, 0, unroll=2)
    for k in range(GROUP):
        outs[min(k, 2)][k // 3] = natural[(me & 3) ^ k]
        outs[3 + k][0] = natural[((me >> 2) * 2) ^ k]


def prepare(place, block):
    slabs = [jax.ShapeDtypeStruct((count, SLAB_ROWS, LANES), f32) for count in (1, 1, 2, 1, 1, 1, 1)]
    return pl.pallas_call(
        prepare_kernel,
        out_shape=slabs,
        in_specs=[in_smem, in_vmem],
        out_specs=[in_vmem] * 7,
        scratch_shapes=[pltpu.VMEM((GROUP, SLAB_ROWS, LANES), f32)],
        compiler_params=pltpu.CompilerParams(vmem_limit_bytes=32 << 20),
        cost_estimate=pl.CostEstimate(flops=0, bytes_accessed=6 << 20, transcendentals=0),
    )(place, block)


def tables_kernel(place, lanes_in, rows_in, forward_in, back_in, table_z, table_y, table_x, table_back, coulomb, sems):
    me = place[0]
    copies = [
        pltpu.make_async_copy(source, target, sems.at[i])
        for i, (source, target) in enumerate(
            ((lanes_in, table_z), (rows_in, table_y), (forward_in.at[me], table_x), (back_in.at[me], table_back))
        )
    ]
    for copy in copies:
        copy.start()
    scale = box_length * box_length / math.pi / (NX * NY * NZ)
    row = lax.broadcasted_iota(jnp.int32, (NY, LANES), 0)
    lane = lax.broadcasted_iota(jnp.int32, (NY, LANES), 1)
    plane = jnp.minimum(row, NY - row) ** 2 + jnp.minimum(lane, NZ - lane) ** 2
    plane = plane.astype(f32)

    def one_plane(x, carry):
        squares = plane + (x * x).astype(f32)
        coulomb[x] = jnp.where((squares > 0.5) & (lane < NZ), scale / jnp.maximum(squares, 1.0), 0.0)
        return carry

    lax.fori_loop(0, NX // 2 + 1, one_plane, 0)
    for copy in copies:
        copy.wait()


def make_tables(place, tables):
    return pl.pallas_call(
        tables_kernel,
        out_shape=[
            jax.ShapeDtypeStruct(tables[0].shape, bf16),
            *[jax.ShapeDtypeStruct(tables[1].shape, bf16)] * 3,
            jax.ShapeDtypeStruct((NX // 2 + 1, NY, LANES), f32),
        ],
        in_specs=[in_smem] + [pl.BlockSpec(memory_space=pl.ANY)] * 4,
        out_specs=[in_vmem] * 5,
        scratch_shapes=[pltpu.SemaphoreType.DMA((4,))],
        compiler_params=pltpu.CompilerParams(vmem_limit_bytes=16 << 20),
        cost_estimate=pl.CostEstimate(flops=0, bytes_accessed=1 << 20, transcendentals=0),
    )(place, *tables)


OWN_PLACES = ((0, 0), (4, 0), (1, 0), (4, 1), (2, 0), (4, 2), (3, 0), (5, 1))
VISITING_PLACES = (
    ((0, 0), (1, 0), (2, 0), (3, 0), (0, 1), (1, 1), (2, 1), (3, 1)),
    tuple((k, 0) for k in range(SLABS)),
)


def pair_kernel(turn, place, mask, *refs):
    places = VISITING_PLACES[turn]
    count = 1 + max(i for i, _ in places)
    own_refs, vis_refs, refs = refs[:6], refs[6 : 6 + count], refs[6 + count :]
    own_slabs = [own_refs[i].at[j] for i, j in OWN_PLACES]
    vis_slabs = [vis_refs[i].at[j] for i, j in places]
    table_z, table_y, table_x, table_back, coulomb, *refs = refs
    if turn:
        before, *refs = refs
        outs, refs = refs[:SLABS], refs[SLABS:]
    else:
        out, *refs = refs
    vis, spectrum = refs
    me = place[0]
    weight = -mask[me & 3, (me >> 2) * 2 + turn].astype(f32)

    def rows_of(step):
        return pl.ds(pl.multiple_of(2 * SLAB_PLANES * step, 8), 2 * SLAB_PLANES)

    def plane_of(y):
        return pl.ds(pl.multiple_of(y * PITCH, 8), NX)

    def columns_of(slabs, step):
        pieces = [slab[rows_of(step), :] for slab in slabs]
        return [
            jnp.concatenate([piece[:SLAB_PLANES] for piece in pieces], axis=0),
            jnp.concatenate([piece[SLAB_PLANES:] for piece in pieces], axis=0),
        ]

    def lane_index():
        return lax.broadcasted_iota(jnp.int32, (NX, LANES), 1)

    def forward(octet, carry):
        lane = lane_index()
        densities = []
        for i in range(3):
            step = 3 * octet + i
            pair = columns_of(vis_slabs, step)
            for j in range(2):
                vis[2 * step + j] = pair[j]
            densities += [a * b for a, b in zip(columns_of(own_slabs, step), pair)]
        for q in range(2):
            first, second, third = densities[3 * q : 3 * q + 3]
            rows = [
                first,
                pltpu.roll(jnp.where(lane >= 96, first, second), 32, 1),
                pltpu.roll(jnp.where(lane >= 64, second, third), 64, 1),
                pltpu.roll(third, 96, 1),
            ]
            done = along_lanes(jnp.concatenate(rows, axis=0), table_z[...])
            for j in range(2):
                both = [done[(2 * j + i) * NX : (2 * j + i + 1) * NX] for i in range(2)]
                both = along_rows(table_x[...], jnp.concatenate(both, axis=1))
                at = 8 * octet + 4 * q + 2 * j
                spectrum[plane_of(at), :] = both[:, :LANES]
                spectrum[plane_of(at + 1), :] = both[:, LANES:]
        return carry

    lax.fori_loop(0, OCTETS, forward, 0, unroll=UNROLL[0])

    def middle(step, carry):
        base = pl.multiple_of(8 * step, 8)
        for j in range(4):
            at = [base + 2 * j, base + 2 * j + 1]
            lines = [pl.ds(i, NY, stride=PITCH) for i in at]
            both = along_rows(table_y[...], jnp.concatenate([spectrum[line, :] for line in lines], axis=1))
            both = both * jnp.concatenate([coulomb[jnp.minimum(i, NX - i)] for i in at], axis=1)
            both = along_rows(table_y[...], both)
            for i, line in enumerate(lines):
                spectrum[line, :] = both[:, i * LANES : (i + 1) * LANES]
        return carry

    lax.fori_loop(0, NX // 8, middle, 0, unroll=UNROLL[1])

    def back(octet, carry):
        lane = lane_index()
        values = []
        for q in range(2):
            rows = []
            for j in range(2):
                at = 8 * octet + 4 * q + 2 * j
                both = along_rows(table_back[...], jnp.concatenate([spectrum[plane_of(at + i), :] for i in range(2)], axis=1))
                rows += [both[:, :LANES], both[:, LANES:]]
            done = along_lanes(jnp.concatenate(rows, axis=0), table_z[...])
            first, second, third, fourth = [done[NX * i : NX * (i + 1)] for i in range(4)]
            second = pltpu.roll(second, 96, 1)
            third = pltpu.roll(third, 64, 1)
            fourth = pltpu.roll(fourth, 32, 1)
            columns = (
                jnp.where(lane < 96, first, second),
                jnp.where(lane < 64, second, third),
                jnp.where(lane < 32, third, fourth),
            )
            for i in range(3):
                at = 6 * octet + 3 * q + i
                value = weight * (columns[i] * vis[at])
                if turn:
                    values.append(before[at] + value)
                else:
                    out[at] = value
        if turn:
            for i in range(3):
                even, odd = values[2 * i : 2 * i + 2]
                for k in range(SLABS):
                    cut = slice(SLAB_PLANES * k, SLAB_PLANES * (k + 1))
                    outs[k][rows_of(3 * octet + i), :] = jnp.concatenate([even[cut], odd[cut]], axis=0)
        return carry

    lax.fori_loop(0, OCTETS, back, 0, unroll=UNROLL[2])


def pair_step(turn, place, mask, own, visiting, tables, before=None):
    extra = [] if before is None else [before]
    whole = jax.ShapeDtypeStruct((COLS, NX, LANES), f32)
    slab = jax.ShapeDtypeStruct((SLAB_ROWS, LANES), f32)
    return pl.pallas_call(
        functools.partial(pair_kernel, turn),
        out_shape=[slab] * SLABS if turn else whole,
        in_specs=[in_smem] * 2 + [in_vmem] * (len(own) + len(visiting) + 5 + len(extra)),
        out_specs=[in_vmem] * SLABS if turn else in_vmem,
        scratch_shapes=[
            pltpu.VMEM((COLS, NX, LANES), f32),
            pltpu.VMEM((NY * PITCH + NX, LANES), f32),
        ],
        compiler_params=pltpu.CompilerParams(vmem_limit_bytes=PAIR_VMEM),
        cost_estimate=pl.CostEstimate(flops=0, bytes_accessed=1 << 20, transcendentals=0),
    )(place, mask, *own, *visiting, *tables, *extra)


def gram_kernel(place, *refs):
    parts, refs = refs[:SLABS], refs[SLABS:]
    own, refs = refs[:3], refs[3:]
    natural, gram = refs
    me = place[0] & 3
    for k in range(GROUP):
        natural[me ^ k] = parts[k][...] + parts[k + GROUP][...]
    for a in range(GROUP):
        for c in range(GROUP):
            terms = own[min(a, 2)][a // 3] * natural[me ^ c]
            terms = jnp.sum(terms.reshape(SLAB_ROWS // 8, 8, LANES), axis=0)
            gram[(me ^ a) * GROUP + (me ^ c)] = jnp.sum(terms, axis=0, keepdims=True)


def layout_kernel(natural, out):
    def two_columns(step, carry):
        rows = pl.ds(pl.multiple_of(2 * SLAB_PLANES * step, 8), 2 * SLAB_PLANES)
        for a in range(GROUP):
            pair = natural[a, rows, :]
            for i in range(2):
                lanes = pl.ds(pl.multiple_of((2 * step + i) * LANES, LANES), LANES)
                out[:, a, lanes] = pair[SLAB_PLANES * i : SLAB_PLANES * (i + 1)]
        return carry

    lax.fori_loop(0, COLS // 2, two_columns, 0, unroll=2)


def finish(place, parts, own):
    natural, gram = pl.pallas_call(
        gram_kernel,
        out_shape=[
            jax.ShapeDtypeStruct((GROUP, SLAB_ROWS, LANES), f32),
            jax.ShapeDtypeStruct((GROUP * GROUP, 1, LANES), f32),
        ],
        in_specs=[in_smem] + [in_vmem] * (SLABS + 3),
        out_specs=[in_vmem] * 2,
        compiler_params=pltpu.CompilerParams(vmem_limit_bytes=32 << 20),
        cost_estimate=pl.CostEstimate(flops=0, bytes_accessed=8 << 20, transcendentals=0),
    )(place, *parts, *own)
    field = pl.pallas_call(
        layout_kernel,
        out_shape=jax.ShapeDtypeStruct((SLAB_PLANES, GROUP, NY * NZ), f32),
        in_specs=[in_vmem],
        out_specs=in_vmem,
        compiler_params=pltpu.CompilerParams(vmem_limit_bytes=32 << 20),
        cost_estimate=pl.CostEstimate(flops=0, bytes_accessed=8 << 20, transcendentals=0),
    )(natural)
    gram = jnp.sum(gram.reshape(GROUP, GROUP, LANES), axis=2) / (NX * NY * NZ)
    gram = gram + to_partner(gram, 1)
    gram = (gram + to_partner(gram, 2)) + (to_partner(gram, 4) + to_partner(gram, 6))
    return field, gram


def to_partner(block, flip):
    return lax.ppermute(block, "grid", [(i, i ^ flip) for i in range(SLABS)])


def to_group(block, distance, flip):
    bands = lax.axis_size("band")
    route = [(b * SLABS + i, (b + distance) % bands * SLABS + (i ^ flip)) for b in range(bands) for i in range(SLABS)]
    return lax.ppermute(block, ("band", "grid"), route)


def after(value, *others):
    return lax.optimization_barrier((value, *others))[0]


def pair_plan(orbitals, pair_mask, cycle_step):
    me = lax.axis_index("grid")
    place = me.astype(jnp.int32).reshape(1)
    cas = cas_table(NX)
    forward_x = jnp.asarray(np.stack([row_table(cas[:, plane_order(d)]) for d in range(SLABS)]))
    back_x = jnp.asarray(np.stack([row_table(cas[plane_order(d), :]) for d in range(SLABS)]))
    fixed = jnp.asarray(lane_table(cas)), jnp.asarray(row_table(cas)), forward_x, back_x
    slabs = prepare(place, jnp.transpose(orbitals, (1, 0, 2)))

    bands = lax.axis_size("band")

    def with_distance(distance, slabs, pair_mask, place, fixed):
        own_out, vis_out = slabs[:3], slabs[3:]
        own_y = to_partner(own_out[0], 4)
        across = to_group(vis_out[2], distance, 4)
        home = to_group(vis_out[0], distance, 0)
        own_next = to_partner(own_out[1], 4)
        own_x = to_partner(own_out[2], 2)
        near = min(distance, bands - distance) == 1
        first = jnp.concatenate([after(home, own_x, own_y), across])
        first_x = to_partner(first, 2)
        across = to_group(after(vis_out[3], first), distance, 4)
        home = to_group(after(vis_out[1], first if near else across), distance, 0)
        tables = make_tables(after(place, first), fixed)
        if near:
            own_far = to_partner(after(own_x, across, own_next, *tables), 4)
            home_x, across_x = to_partner(home, 2), to_partner(across, 2)
            ready, last = home, home_x
        else:
            own_far = to_partner(after(own_x, own_next, *tables), 4)
            ready = last = across
        crossing = jnp.concatenate([after(own_out[1], ready if not near else first), own_x[1:], own_next])
        crossed, far_crossed = to_partner(crossing, 1), to_partner(after(own_far, last), 1)
        first_core, beside_core = to_partner(after(first, ready), 1), to_partner(after(first_x, ready), 1)
        own = [own_out[0], own_x, own_y, own_far, crossed, far_crossed]
        visiting = [first, first_core, first_x, beside_core]
        total = pair_step(0, place, pair_mask, own, visiting, tables)
        if not near:
            home_x, across_x = to_partner(after(home, total), 2), to_partner(across, 2)
        cores = [to_partner(slab, 1) for slab in (home, home_x, across)]
        cores.append(to_partner(after(across_x, total), 1))
        visiting = [home, cores[0], home_x, cores[1], across, cores[2], across_x, cores[3]]
        parts = pair_step(1, place, pair_mask, own, visiting, tables, total)
        parts = [parts[0]] + [to_partner(parts[k], k) for k in range(1, SLABS)]
        return finish(place, parts, own_out)

    field, gram = lax.switch(
        cycle_step - 1,
        [functools.partial(with_distance, distance) for distance in range(1, bands)],
        slabs,
        pair_mask,
        place,
        fixed,
    )
    return jnp.transpose(field, (1, 0, 2)), gram


def shards(orbitals, pair_mask, cycle_step):
    if lax.axis_size("grid") == SLABS and orbitals.shape[0] == GROUP:
        return pair_plan(orbitals, pair_mask, cycle_step)
    return slab_plan(orbitals, pair_mask, cycle_step)


def solution(mesh):
    return jax.shard_map(
        shards,
        mesh=mesh,
        in_specs=(P("band", "grid", None), P("band", None), P()),
        out_specs=(P("band", "grid", None), P("band", None)),
        check_vma=False,
    )
```

```python
import functools
import math

import jax
import jax.numpy as jnp
import ml_dtypes
import numpy as np
from jax import lax
from jax.experimental import pallas as pl
from jax.experimental.pallas import tpu as pltpu
from jax.sharding import PartitionSpec as P

NX = 96
NY = 96
NZ = 96
LANES = 128


box_length = 16.0
highest = lax.Precision.HIGHEST


def passed_along(block, axis, distance):
    devices = range(lax.axis_size(axis))
    route = [((i - distance) % len(devices), i) for i in devices]
    return lax.ppermute(block, axis, route)


def hartley_table(length):
    index = jnp.arange(length, dtype=jnp.int32)
    product = index[:, None] * index[None, :] % length
    angle = product.astype(jnp.float32) * (2.0 * math.pi / length)
    return jnp.cos(angle) + jnp.sin(angle)


def folded(index, length):
    return jnp.where(index * 2 >= length, index - length, index).astype(jnp.float32)


def across_planes(field, table_y, table_z):
    count = field.shape[0]
    planes = field.shape[1]
    shaped = field.reshape(count * planes * NY, NZ)
    shaped = jnp.matmul(shaped, table_z, precision=highest)
    shaped = shaped.reshape(count * planes, NY, NZ)
    shaped = jnp.matmul(table_y, shaped, precision=highest)
    return shaped.reshape(count, planes, NY * NZ)


def slab_plan(orbitals, pair_mask, cycle_step):
    orbit_count = orbitals.shape[0]
    planes = orbitals.shape[1]
    grid_count = lax.axis_size("grid")
    slab_rows = NY // grid_count

    def one_hop(turn, block):
        return passed_along(block, "band", 1)

    visiting = lax.fori_loop(0, cycle_step, one_hop, orbitals)
    table_x = hartley_table(NX)
    table_y = hartley_table(NY)
    table_z = hartley_table(NZ)
    row_index = lax.axis_index("grid") * slab_rows + jnp.arange(slab_rows, dtype=jnp.int32)
    freq_x = folded(jnp.arange(NX, dtype=jnp.int32), NX)
    freq_y = folded(row_index, NY)
    freq_z = folded(jnp.arange(NZ, dtype=jnp.int32), NZ)
    squares = freq_x[:, None, None] ** 2 + freq_y[None, :, None] ** 2 + freq_z[None, None, :] ** 2
    coulomb = box_length * box_length / math.pi / (NX * NY * NZ)
    kernel = jnp.where(squares > 0.5, coulomb / jnp.maximum(squares, 1.0), jnp.float32(0.0))
    kernel = kernel.reshape(NX, slab_rows * NZ)

    def solve_items(spectra):
        along = jnp.matmul(table_x, spectra, precision=highest) * kernel
        along = jnp.matmul(table_x, along, precision=highest)
        return lax.all_to_all(along, "grid", split_axis=1, concat_axis=2, tiled=True)

    mask_float = pair_mask.astype(jnp.float32).reshape(
        orbit_count // orbit_count, orbit_count, orbit_count
    )
    own_rows = orbitals.reshape(orbit_count // orbit_count, orbit_count, planes, NY * NZ)

    def one_group(carry, inputs):
        rows, weights = inputs
        density = (rows[:, None] * visiting[None]).reshape(
            orbit_count * orbit_count, planes, NY * NZ
        )
        spectra = across_planes(density, table_y, table_z)
        potential = solve_items(
            lax.all_to_all(spectra, "grid", split_axis=2, concat_axis=1, tiled=True)
        )
        potential = across_planes(potential, table_y, table_z)
        potential = potential.reshape(orbit_count, orbit_count, planes, NY * NZ)
        field = -jnp.einsum("aj,ajxr->axr", weights, potential * visiting[None], precision=highest)
        return (carry, field)

    start_carry = jnp.zeros((), jnp.float32)
    _, fields = lax.scan(one_group, start_carry, (own_rows, mask_float))
    exchange_field = fields.reshape(orbit_count, planes, NY * NZ)
    local_terms = jnp.einsum("axr,cxr->ac", orbitals, exchange_field, precision=highest) / (
        NX * NY * NZ
    )
    projection = lax.psum(local_terms, "grid")
    return (exchange_field, projection)


SLABS = 8
GROUP = 4
SLAB_PLANES = NX // SLABS
COLS = NY * NZ // LANES
SLAB_ROWS = SLAB_PLANES * COLS
OCTETS = NY // 8
PITCH = NX + 8
UNROLL = (6, 4, 4)
PAIR_VMEM = 36 << 20

bf16 = jnp.bfloat16
f32 = jnp.float32
in_vmem = pl.BlockSpec(memory_space=pltpu.VMEM)
in_smem = pl.BlockSpec(memory_space=pltpu.SMEM)


def high_low(table):
    high = table.astype(ml_dtypes.bfloat16)
    return high, (table - high.astype(np.float64)).astype(ml_dtypes.bfloat16)


def cas_table(length):
    index = np.arange(length)
    angle = (index[:, None] * index[None, :] % length) * (2.0 * np.pi / length)
    return np.cos(angle) + np.sin(angle)


def lane_table(table):
    high, low = high_low(table)
    out = np.zeros((2 * LANES, 2 * LANES), high.dtype)
    for row in (0, LANES):
        out[row : row + NZ, :NZ] = high
        out[row : row + NZ, LANES : LANES + NZ] = low
    return out


def row_table(table):
    high, low = high_low(table)
    return np.concatenate([np.concatenate([high, high], 1), np.concatenate([low, low], 1)], 0)


def plane_order(device):
    return np.concatenate([np.arange(SLAB_PLANES) + SLAB_PLANES * (device ^ k) for k in range(SLABS)])


def split(value):
    high = value.astype(bf16)
    return high, (value - high.astype(f32)).astype(bf16)


def product(left, right):
    return lax.dot_general(left, right, (((1,), (0,)), ((), ())), preferred_element_type=f32)


def along_lanes(value, table):
    both = product(jnp.concatenate(split(value), axis=1), table)
    return both[:, :LANES] + both[:, LANES:]


def along_rows(table, value):
    both = product(table, jnp.concatenate(split(value), axis=0))
    half = both.shape[0] // 2
    return both[:half] + both[half:]


def prepare_kernel(place, block, *refs):
    outs, natural = refs[:-1], refs[-1]
    me = place[0]

    def two_columns(step, carry):
        for a in range(GROUP):
            pair = [block[:, a, pl.ds(pl.multiple_of((2 * step + i) * LANES, LANES), LANES)] for i in range(2)]
            natural[a, pl.ds(pl.multiple_of(2 * SLAB_PLANES * step, 8), 2 * SLAB_PLANES), :] = jnp.concatenate(pair, 0)
        return carry

    lax.fori_loop(0, COLS // 2, two_columns, 0, unroll=2)
    for k in range(GROUP):
        outs[min(k, 2)][k // 3] = natural[(me & 3) ^ k]
        outs[3 + k][0] = natural[((me >> 2) * 2) ^ k]


def prepare(place, block):
    slabs = [jax.ShapeDtypeStruct((count, SLAB_ROWS, LANES), f32) for count in (1, 1, 2, 1, 1, 1, 1)]
    return pl.pallas_call(
        prepare_kernel,
        out_shape=slabs,
        in_specs=[in_smem, in_vmem],
        out_specs=[in_vmem] * 7,
        scratch_shapes=[pltpu.VMEM((GROUP, SLAB_ROWS, LANES), f32)],
        compiler_params=pltpu.CompilerParams(vmem_limit_bytes=32 << 20),
        cost_estimate=pl.CostEstimate(flops=0, bytes_accessed=6 << 20, transcendentals=0),
    )(place, block)


def tables_kernel(place, lanes_in, rows_in, forward_in, back_in, table_z, table_y, table_x, table_back, coulomb, sems):
    me = place[0]
    copies = [
        pltpu.make_async_copy(source, target, sems.at[i])
        for i, (source, target) in enumerate(
            ((lanes_in, table_z), (rows_in, table_y), (forward_in.at[me], table_x), (back_in.at[me], table_back))
        )
    ]
    for copy in copies:
        copy.start()
    scale = box_length * box_length / math.pi / (NX * NY * NZ)
    row = lax.broadcasted_iota(jnp.int32, (NY, LANES), 0)
    lane = lax.broadcasted_iota(jnp.int32, (NY, LANES), 1)
    plane = jnp.minimum(row, NY - row) ** 2 + jnp.minimum(lane, NZ - lane) ** 2
    plane = plane.astype(f32)

    def one_plane(x, carry):
        squares = plane + (x * x).astype(f32)
        coulomb[x] = jnp.where((squares > 0.5) & (lane < NZ), scale / jnp.maximum(squares, 1.0), 0.0)
        return carry

    lax.fori_loop(0, NX // 2 + 1, one_plane, 0)
    for copy in copies:
        copy.wait()


def make_tables(place, tables):
    return pl.pallas_call(
        tables_kernel,
        out_shape=[
            jax.ShapeDtypeStruct(tables[0].shape, bf16),
            *[jax.ShapeDtypeStruct(tables[1].shape, bf16)] * 3,
            jax.ShapeDtypeStruct((NX // 2 + 1, NY, LANES), f32),
        ],
        in_specs=[in_smem] + [pl.BlockSpec(memory_space=pl.ANY)] * 4,
        out_specs=[in_vmem] * 5,
        scratch_shapes=[pltpu.SemaphoreType.DMA((4,))],
        compiler_params=pltpu.CompilerParams(vmem_limit_bytes=16 << 20),
        cost_estimate=pl.CostEstimate(flops=0, bytes_accessed=1 << 20, transcendentals=0),
    )(place, *tables)


OWN_PLACES = ((0, 0), (4, 0), (1, 0), (4, 1), (2, 0), (4, 2), (3, 0), (5, 1))
VISITING_PLACES = (
    ((0, 0), (1, 0), (2, 0), (3, 0), (0, 1), (1, 1), (2, 1), (3, 1)),
    tuple((k, 0) for k in range(SLABS)),
)


def pair_kernel(turn, place, mask, *refs):
    places = VISITING_PLACES[turn]
    count = 1 + max(i for i, _ in places)
    own_refs, vis_refs, refs = refs[:6], refs[6 : 6 + count], refs[6 + count :]
    own_slabs = [own_refs[i].at[j] for i, j in OWN_PLACES]
    vis_slabs = [vis_refs[i].at[j] for i, j in places]
    table_z, table_y, table_x, table_back, coulomb, *refs = refs
    if turn:
        before, *refs = refs
        outs, refs = refs[:SLABS], refs[SLABS:]
    else:
        out, *refs = refs
    vis, spectrum = refs
    me = place[0]
    weight = -mask[me & 3, (me >> 2) * 2 + turn].astype(f32)

    def rows_of(step):
        return pl.ds(pl.multiple_of(2 * SLAB_PLANES * step, 8), 2 * SLAB_PLANES)

    def plane_of(y):
        return pl.ds(pl.multiple_of(y * PITCH, 8), NX)

    def columns_of(slabs, step):
        pieces = [slab[rows_of(step), :] for slab in slabs]
        return [
            jnp.concatenate([piece[:SLAB_PLANES] for piece in pieces], axis=0),
            jnp.concatenate([piece[SLAB_PLANES:] for piece in pieces], axis=0),
        ]

    def lane_index():
        return lax.broadcasted_iota(jnp.int32, (NX, LANES), 1)

    def forward(octet, carry):
        lane = lane_index()
        densities = []
        for i in range(3):
            step = 3 * octet + i
            pair = columns_of(vis_slabs, step)
            for j in range(2):
                vis[2 * step + j] = pair[j]
            densities += [a * b for a, b in zip(columns_of(own_slabs, step), pair)]
        for q in range(2):
            first, second, third = densities[3 * q : 3 * q + 3]
            rows = [
                first,
                pltpu.roll(jnp.where(lane >= 96, first, second), 32, 1),
                pltpu.roll(jnp.where(lane >= 64, second, third), 64, 1),
                pltpu.roll(third, 96, 1),
            ]
            done = along_lanes(jnp.concatenate(rows, axis=0), table_z[...])
            for j in range(2):
                both = [done[(2 * j + i) * NX : (2 * j + i + 1) * NX] for i in range(2)]
                both = along_rows(table_x[...], jnp.concatenate(both, axis=1))
                at = 8 * octet + 4 * q + 2 * j
                spectrum[plane_of(at), :] = both[:, :LANES]
                spectrum[plane_of(at + 1), :] = both[:, LANES:]
        return carry

    lax.fori_loop(0, OCTETS, forward, 0, unroll=UNROLL[0])

    def middle(step, carry):
        base = pl.multiple_of(8 * step, 8)
        for j in range(4):
            at = [base + 2 * j, base + 2 * j + 1]
            lines = [pl.ds(i, NY, stride=PITCH) for i in at]
            both = along_rows(table_y[...], jnp.concatenate([spectrum[line, :] for line in lines], axis=1))
            both = both * jnp.concatenate([coulomb[jnp.minimum(i, NX - i)] for i in at], axis=1)
            both = along_rows(table_y[...], both)
            for i, line in enumerate(lines):
                spectrum[line, :] = both[:, i * LANES : (i + 1) * LANES]
        return carry

    lax.fori_loop(0, NX // 8, middle, 0, unroll=UNROLL[1])

    def back(octet, carry):
        lane = lane_index()
        values = []
        for q in range(2):
            rows = []
            for j in range(2):
                at = 8 * octet + 4 * q + 2 * j
                both = along_rows(table_back[...], jnp.concatenate([spectrum[plane_of(at + i), :] for i in range(2)], axis=1))
                rows += [both[:, :LANES], both[:, LANES:]]
            done = along_lanes(jnp.concatenate(rows, axis=0), table_z[...])
            first, second, third, fourth = [done[NX * i : NX * (i + 1)] for i in range(4)]
            second = pltpu.roll(second, 96, 1)
            third = pltpu.roll(third, 64, 1)
            fourth = pltpu.roll(fourth, 32, 1)
            columns = (
                jnp.where(lane < 96, first, second),
                jnp.where(lane < 64, second, third),
                jnp.where(lane < 32, third, fourth),
            )
            for i in range(3):
                at = 6 * octet + 3 * q + i
                value = weight * (columns[i] * vis[at])
                if turn:
                    values.append(before[at] + value)
                else:
                    out[at] = value
        if turn:
            for i in range(3):
                even, odd = values[2 * i : 2 * i + 2]
                for k in range(SLABS):
                    cut = slice(SLAB_PLANES * k, SLAB_PLANES * (k + 1))
                    outs[k][rows_of(3 * octet + i), :] = jnp.concatenate([even[cut], odd[cut]], axis=0)
        return carry

    lax.fori_loop(0, OCTETS, back, 0, unroll=UNROLL[2])


def pair_step(turn, place, mask, own, visiting, tables, before=None):
    extra = [] if before is None else [before]
    whole = jax.ShapeDtypeStruct((COLS, NX, LANES), f32)
    slab = jax.ShapeDtypeStruct((SLAB_ROWS, LANES), f32)
    return pl.pallas_call(
        functools.partial(pair_kernel, turn),
        out_shape=[slab] * SLABS if turn else whole,
        in_specs=[in_smem] * 2 + [in_vmem] * (len(own) + len(visiting) + 5 + len(extra)),
        out_specs=[in_vmem] * SLABS if turn else in_vmem,
        scratch_shapes=[
            pltpu.VMEM((COLS, NX, LANES), f32),
            pltpu.VMEM((NY * PITCH + NX, LANES), f32),
        ],
        compiler_params=pltpu.CompilerParams(vmem_limit_bytes=PAIR_VMEM),
        cost_estimate=pl.CostEstimate(flops=0, bytes_accessed=1 << 20, transcendentals=0),
    )(place, mask, *own, *visiting, *tables, *extra)


def gram_kernel(place, *refs):
    parts, refs = refs[:SLABS], refs[SLABS:]
    own, refs = refs[:3], refs[3:]
    natural, gram = refs
    me = place[0] & 3
    for k in range(GROUP):
        natural[me ^ k] = parts[k][...] + parts[k + GROUP][...]
    for a in range(GROUP):
        for c in range(GROUP):
            terms = own[min(a, 2)][a // 3] * natural[me ^ c]
            terms = jnp.sum(terms.reshape(SLAB_ROWS // 8, 8, LANES), axis=0)
            gram[(me ^ a) * GROUP + (me ^ c)] = jnp.sum(terms, axis=0, keepdims=True)


def layout_kernel(natural, out):
    def two_columns(step, carry):
        rows = pl.ds(pl.multiple_of(2 * SLAB_PLANES * step, 8), 2 * SLAB_PLANES)
        for a in range(GROUP):
            pair = natural[a, rows, :]
            for i in range(2):
                lanes = pl.ds(pl.multiple_of((2 * step + i) * LANES, LANES), LANES)
                out[:, a, lanes] = pair[SLAB_PLANES * i : SLAB_PLANES * (i + 1)]
        return carry

    lax.fori_loop(0, COLS // 2, two_columns, 0, unroll=2)


def finish(place, parts, own):
    natural, gram = pl.pallas_call(
        gram_kernel,
        out_shape=[
            jax.ShapeDtypeStruct((GROUP, SLAB_ROWS, LANES), f32),
            jax.ShapeDtypeStruct((GROUP * GROUP, 1, LANES), f32),
        ],
        in_specs=[in_smem] + [in_vmem] * (SLABS + 3),
        out_specs=[in_vmem] * 2,
        compiler_params=pltpu.CompilerParams(vmem_limit_bytes=32 << 20),
        cost_estimate=pl.CostEstimate(flops=0, bytes_accessed=8 << 20, transcendentals=0),
    )(place, *parts, *own)
    field = pl.pallas_call(
        layout_kernel,
        out_shape=jax.ShapeDtypeStruct((SLAB_PLANES, GROUP, NY * NZ), f32),
        in_specs=[in_vmem],
        out_specs=in_vmem,
        compiler_params=pltpu.CompilerParams(vmem_limit_bytes=32 << 20),
        cost_estimate=pl.CostEstimate(flops=0, bytes_accessed=8 << 20, transcendentals=0),
    )(natural)
    gram = jnp.sum(gram.reshape(GROUP, GROUP, LANES), axis=2) / (NX * NY * NZ)
    gram = gram + to_partner(gram, 1)
    gram = (gram + to_partner(gram, 2)) + (to_partner(gram, 4) + to_partner(gram, 6))
    return field, gram


def to_partner(block, flip):
    return lax.ppermute(block, "grid", [(i, i ^ flip) for i in range(SLABS)])


def to_group(block, distance, flip):
    bands = lax.axis_size("band")
    route = [(b * SLABS + i, (b + distance) % bands * SLABS + (i ^ flip)) for b in range(bands) for i in range(SLABS)]
    return lax.ppermute(block, ("band", "grid"), route)


def after(value, *others):
    return lax.optimization_barrier((value, *others))[0]


def pair_plan(orbitals, pair_mask, cycle_step):
    me = lax.axis_index("grid")
    place = me.astype(jnp.int32).reshape(1)
    cas = cas_table(NX)
    forward_x = jnp.asarray(np.stack([row_table(cas[:, plane_order(d)]) for d in range(SLABS)]))
    back_x = jnp.asarray(np.stack([row_table(cas[plane_order(d), :]) for d in range(SLABS)]))
    fixed = jnp.asarray(lane_table(cas)), jnp.asarray(row_table(cas)), forward_x, back_x
    slabs = prepare(place, jnp.transpose(orbitals, (1, 0, 2)))

    bands = lax.axis_size("band")

    def with_distance(distance, slabs, pair_mask, place, fixed):
        own_out, vis_out = slabs[:3], slabs[3:]
        own_y = to_partner(own_out[0], 4)
        across = to_group(vis_out[2], distance, 4)
        home = to_group(vis_out[0], distance, 0)
        own_next = to_partner(own_out[1], 4)
        own_x = to_partner(own_out[2], 2)
        near = min(distance, bands - distance) == 1
        first = jnp.concatenate([after(home, own_x, own_y), across])
        first_x = to_partner(first, 2)
        across = to_group(after(vis_out[3], first), distance, 4)
        home = to_group(after(vis_out[1], first), distance, 0)
        home_x, across_x = to_partner(home, 2), to_partner(across, 2)
        tables = make_tables(after(place, first), fixed)
        if near:
            own_far = to_partner(after(own_x, across, own_next, *tables), 4)
            ready, last = home, home_x
        else:
            own_far = to_partner(after(own_x, own_next, *tables), 4)
            ready = last = home
        crossing = jnp.concatenate([after(own_out[1], ready if not near else first), own_x[1:], own_next])
        crossed, far_crossed = to_partner(crossing, 1), to_partner(after(own_far, last), 1)
        first_core, beside_core = to_partner(after(first, ready), 1), to_partner(after(first_x, ready), 1)
        own = [own_out[0], own_x, own_y, own_far, crossed, far_crossed]
        visiting = [first, first_core, first_x, beside_core]
        total = pair_step(0, place, pair_mask, own, visiting, tables)
        if not near:
            home_x, across = after(home_x, total), after(across, total)
            across_x = to_partner(across, 2)
        cores = [to_partner(slab, 1) for slab in (home, home_x, across)]
        cores.append(to_partner(after(across_x, total), 1))
        visiting = [home, cores[0], home_x, cores[1], across, cores[2], across_x, cores[3]]
        parts = pair_step(1, place, pair_mask, own, visiting, tables, total)
        parts = [parts[0]] + [to_partner(parts[k], k) for k in range(1, SLABS)]
        return finish(place, parts, own_out)

    field, gram = lax.switch(
        cycle_step - 1,
        [functools.partial(with_distance, distance) for distance in range(1, bands)],
        slabs,
        pair_mask,
        place,
        fixed,
    )
    return jnp.transpose(field, (1, 0, 2)), gram


def shards(orbitals, pair_mask, cycle_step):
    if lax.axis_size("grid") == SLABS and orbitals.shape[0] == GROUP:
        return pair_plan(orbitals, pair_mask, cycle_step)
    return slab_plan(orbitals, pair_mask, cycle_step)


def solution(mesh):
    return jax.shard_map(
        shards,
        mesh=mesh,
        in_specs=(P("band", "grid", None), P("band", None), P()),
        out_specs=(P("band", "grid", None), P("band", None)),
        check_vma=False,
    )
```
